128 devices in a mesh: block: 32 (over z, x, core), grp: 4 (over y).
Axes of the slice: x: 4, y: 4, z: 4, core: 2. Of those that a mesh axis runs over, the one named last changes fastest.
Arguments:
- features: bfloat16 [512, 256, 128], P(('block', 'grp')), may hold values from -6 to 6
- point_counts: int32 [512], P(('block', 'grp')), may hold values from 128 to 256, as said below
- kernel_weights: bfloat16 [15, 128, 128], replicated, may hold values from -0.015625 to 0.015625
- influence: bfloat16 [1024, 15, 256, 256], P(('block', 'grp')), may hold values from 0 to 1
- pair_list: int32 [1024, 2], P(('block', 'grp')), may hold values from 0 to 511, as said below
- pair_counts: int32 [128], P(('block', 'grp')), may hold values from 1 to 8, as said below
- cotangent: bfloat16 [512, 256, 128], P(('block', 'grp')), may hold values from -6 to 6
Outputs:
- activated: bfloat16 [512, 256, 128], P(('block', 'grp'))
- grad_features: bfloat16 [512, 256, 128], P(('block', 'grp'))
- grad_weights: float32 [15, 128, 128], replicated
The draws below stay inside these ranges and needn't reach their ends.
Inputs may be any that keep to these rules, and one draw needn't show every extreme that they name: `pair_list`: block x lives on device x // 4, and device d has block index d // 4 and grp index d % 4. Column 0 is below 4; the second block of every slot lives on a device whose block index differs from the slot's device's by at most one; any grp index may occur. `pair_counts`: slots at or beyond a device's count are unused. Some device uses all 8 slots. `point_counts`: the real points of a block are its first rows; the others are padding.
All inputs are finite; a program needn't handle non-finite values.
Results may differ from the reference program's by a relative error of at most 0.0063.
Values may be sent and summed in bfloat16 or wider, within the bound.
No kernel may reach another device: no remote copies, remote signals or barrier semaphores. Data moves between devices by JAX's collectives and lax.ppermute only.
A program may use at most 128 MiB of HBM per device.

```python
import math
import jax
import jax.numpy as jnp
from jax import lax

C = 128
K = 15
P_SIZE = 256
BLK_DEV = 4
PAIR_DEV = 8
BLOCKS = 512
SLOTS = 1024
POINTS = 131072
N_BLOCK = 32
N_GRP = 4


def draw_pair_list(key, part):
    total = N_BLOCK * N_GRP * PAIR_DEV
    keys = jax.random.split(key, 4)
    device = jnp.arange(total, dtype=jnp.int32) // PAIR_DEV
    column = device // N_GRP
    first = jax.random.randint(keys[0], (total,), 0, BLK_DEV, dtype=jnp.int32)
    offset = jax.random.randint(keys[1], (total,), -1, 2, dtype=jnp.int32)
    target = jnp.clip(column + offset, 0, N_BLOCK - 1)
    region = jax.random.randint(keys[2], (total,), 0, N_GRP, dtype=jnp.int32)
    local = jax.random.randint(keys[3], (total,), 0, BLK_DEV, dtype=jnp.int32)
    second = (target * N_GRP + region) * BLK_DEV + local
    return jnp.stack([first, second], axis=1).astype(jnp.int32)


def draw_pair_counts(key, part):
    devices_all = N_BLOCK * N_GRP
    keys = jax.random.split(key, 3)
    base = jax.random.randint(keys[0], (devices_all,), min(3, PAIR_DEV), min(6, PAIR_DEV) + 1, dtype=jnp.int32)
    busy = jax.random.randint(keys[1], (devices_all,), 0, 8, dtype=jnp.int32) == 0
    chosen = jax.random.randint(keys[2], (), 0, devices_all, dtype=jnp.int32)
    forced = jnp.arange(devices_all, dtype=jnp.int32) == chosen
    return jnp.where(busy | forced, PAIR_DEV, base).astype(jnp.int32)


def draw_point_counts(key, part):
    keys = jax.random.split(key, 3)
    counts = jax.random.randint(keys[0], (BLOCKS,), P_SIZE // 2, P_SIZE + 1, dtype=jnp.int32)
    full_at = jax.random.randint(keys[1], (), 0, BLOCKS, dtype=jnp.int32)
    half_at = (full_at + 1 + jax.random.randint(keys[2], (), 0, BLOCKS - 1, dtype=jnp.int32)) % BLOCKS
    index = jnp.arange(BLOCKS, dtype=jnp.int32)
    counts = jnp.where(index == full_at, P_SIZE, counts)
    counts = jnp.where(index == half_at, P_SIZE // 2, counts)
    return counts.astype(jnp.int32)


def steps_of(key, shape, pieces, least, largest):
    def one(axis_at, blocks):
        draws = jax.random.uniform(jax.random.fold_in(jax.random.fold_in(key, 6), axis_at), (blocks,), jnp.float32, least / len(pieces), largest / len(pieces))
        return jnp.repeat(jnp.exp(draws), shape[axis_at] // blocks).reshape((-1,) + (1,) * (len(shape) - axis_at - 1))

    level = one(*pieces[0])
    for cut in pieces[1:]:
        level = level * one(*cut)
    return level


def bell_draw(own_key, extent, spread, limit, cuts=(), kind=jnp.bfloat16):
    values = jax.random.normal(own_key, extent, jnp.float32) * spread
    if len(cuts) > 0:
        values = steps_of(own_key, extent, cuts, -0.22, 0.18) * values
    return jnp.clip(values, min=-limit, max=limit).astype(kind)


def setup_inputs(seed: int = 0) -> dict:
    key_list = jax.random.split(jax.random.key(seed), 8)
    features = bell_draw(key_list[0], (BLOCKS, P_SIZE, C), 1.0, 6.0, ((0, 128),))
    point_counts = draw_point_counts(jax.random.fold_in(key_list[7], 71), 0)
    kernel_weights = bell_draw(key_list[2], (K, C, C), (K * C * P_SIZE // 3) ** -0.5, 0.015625)
    influence = jnp.clip(1.0 * jax.random.uniform(key_list[3], (SLOTS, K, P_SIZE, P_SIZE), jnp.float32) ** steps_of(key_list[3], (SLOTS, K, P_SIZE, P_SIZE), ((0, 128),), -0.2, 0.2), 0.0, 1.0).astype(jnp.bfloat16)
    pair_list = draw_pair_list(jax.random.fold_in(key_list[7], 71), 0)
    pair_counts = draw_pair_counts(jax.random.fold_in(key_list[7], 71), 0)
    cotangent = bell_draw(key_list[6], (BLOCKS, P_SIZE, C), 1.0, 6.0, ((0, 128),))
    return dict(features=features, point_counts=point_counts, kernel_weights=kernel_weights, influence=influence, pair_list=pair_list, pair_counts=pair_counts, cotangent=cotangent)


def gather_terms(tile, rows):
    out = jnp.einsum('kij,jc->ikc', tile.astype(jnp.float32), rows.astype(jnp.float32))
    return out.astype(jnp.bfloat16).reshape(P_SIZE, K * C)

def scatter_terms(tile, rows):
    out = jnp.einsum('kij,ic->jkc', tile.astype(jnp.float32), rows.astype(jnp.float32))
    return out.astype(jnp.bfloat16).reshape(P_SIZE, K * C)

def reference(features, point_counts, kernel_weights, influence, pair_list, pair_counts, cotangent):
    valid = (jnp.arange(P_SIZE, dtype=jnp.int32)[None, :] < point_counts[:, None])[..., None]
    masked = jnp.where(valid, features, jnp.zeros_like(features))
    direct = kernel_weights.reshape(K * C, C)
    mirrored = kernel_weights[::-1].reshape(K * C, C)
    slot_ids = jnp.arange(SLOTS, dtype=jnp.int32)

    def locate(pair, slot):
        device = (slot // PAIR_DEV).astype(jnp.int32)
        active = slot - device * PAIR_DEV < pair_counts[device]
        first = (device * BLK_DEV + pair[0]).astype(jnp.int32)
        second = pair[1].astype(jnp.int32)
        return (active, first, second)

    def forward(total, item):
        tile, pair, slot = item
        active, first, second = locate(pair, slot)

        def work(total):
            to_first = jnp.dot(gather_terms(tile, masked[second]), direct, preferred_element_type=jnp.float32)
            to_second = jnp.dot(scatter_terms(tile, masked[first]), mirrored, preferred_element_type=jnp.float32)
            total = total.at[first].add(to_first)
            return total.at[second].add(to_second)
        return (lax.cond(active, work, lambda total: total, total), None)
    start = jnp.zeros((BLOCKS, P_SIZE, C), jnp.float32)
    total, _ = lax.scan(forward, start, (influence, pair_list, slot_ids))
    pre = jnp.where(valid, total, jnp.zeros_like(total))
    activated = jax.nn.silu(pre).astype(jnp.bfloat16)
    sig = jax.nn.sigmoid(pre)
    slope = sig * (1.0 + pre * (1.0 - sig))
    upstream = jnp.where(valid, cotangent.astype(jnp.float32) * slope, jnp.zeros_like(pre)).astype(jnp.bfloat16)

    def backward(carry, item):
        tile, pair, slot = item
        active, first, second = locate(pair, slot)

        def work(carry):
            grad_rows, grad_direct, grad_mirror = carry
            near_terms = gather_terms(tile, masked[second])
            own_terms = scatter_terms(tile, masked[first])
            up_first = upstream[first]
            up_second = upstream[second]
            grad_direct = grad_direct + jnp.dot(near_terms.T, up_first, preferred_element_type=jnp.float32)
            grad_mirror = grad_mirror + jnp.dot(own_terms.T, up_second, preferred_element_type=jnp.float32)
            back_near = jnp.dot(up_first, direct.T, preferred_element_type=jnp.float32).astype(jnp.bfloat16).reshape(P_SIZE, K, C)
            back_own = jnp.dot(up_second, mirrored.T, preferred_element_type=jnp.float32).astype(jnp.bfloat16).reshape(P_SIZE, K, C)
            to_second = jnp.einsum('kij,ikc->jc', tile.astype(jnp.float32), back_near.astype(jnp.float32))
            to_first = jnp.einsum('kij,jkc->ic', tile.astype(jnp.float32), back_own.astype(jnp.float32))
            grad_rows = grad_rows.at[second].add(to_second)
            grad_rows = grad_rows.at[first].add(to_first)
            return (grad_rows, grad_direct, grad_mirror)
        return (lax.cond(active, work, lambda carry: carry, carry), None)
    empty = jnp.zeros((K * C, C), jnp.float32)
    carry, _ = lax.scan(backward, (start, empty, empty), (influence, pair_list, slot_ids))
    grad_rows, grad_direct, grad_mirror = carry
    grad_features = jnp.where(valid, grad_rows, jnp.zeros_like(grad_rows)).astype(jnp.bfloat16)
    grad_weights = (grad_direct.reshape(K, C, C) + grad_mirror.reshape(K, C, C)[::-1]) * (1.0 / math.sqrt(POINTS))
    return (activated, grad_features, grad_weights)
```

```python
import functools
import math

import jax
import jax.numpy as jnp
from jax import lax
from jax.experimental import pallas as pl
from jax.experimental.pallas import tpu as pltpu
from jax.sharding import PartitionSpec as P

BF16 = jnp.bfloat16
F32 = jnp.float32
VMEM_LIMIT = 48 * 1024 * 1024


def dot(a, b):
    return jnp.dot(a, b, preferred_element_type=F32)


def struct(shape, dtype):
    return jax.ShapeDtypeStruct(shape, dtype)


def whole(shape):
    return pl.BlockSpec(shape, lambda *_: (0,) * len(shape))


def slot_of(s, counts):
    return jnp.minimum(s, counts[0] - 1)


def per_slot(shape):
    zeros = (0,) * (len(shape) - 1)
    return pl.BlockSpec(shape, lambda s, counts, *_: (slot_of(s, counts),) + zeros)


def call(kernel, grid, prefetch, in_specs, out_specs, out_shape, scratch, name, flops=0, size=0):
    return pl.pallas_call(
        kernel,
        grid_spec=pltpu.PrefetchScalarGridSpec(
            num_scalar_prefetch=prefetch,
            grid=grid,
            in_specs=in_specs,
            out_specs=out_specs,
            scratch_shapes=scratch,
        ),
        out_shape=out_shape,
        compiler_params=pltpu.CompilerParams(vmem_limit_bytes=VMEM_LIMIT),
        cost_estimate=pl.CostEstimate(flops=flops, bytes_accessed=size, transcendentals=0),
        name=name,
    )


def own_kernel(counts, pairs, m_ref, w_ref, h_ref, out_ref, mt_ref, wmt_ref, yt):
    kernels, points = h_ref.shape[1], h_ref.shape[2]
    s = pl.program_id(0)

    @pl.when(s == 0)
    def _():
        for k in range(kernels):
            wmt_ref[k] = w_ref[kernels - 1 - k].T
        for a in range(m_ref.shape[0]):
            mt_ref[a] = m_ref[a].T
            mt = mt_ref[a]
            for k in range(kernels):
                yt[a, :, k * points : (k + 1) * points] = dot(wmt_ref[k], mt).astype(BF16)

    @pl.when(s < counts[0])
    def _():
        a = pairs[s, 0]
        out_ref[0] = dot(yt[a], h_ref[0].reshape(kernels * points, points)).astype(BF16)


def near_select(second, l_ref, c_ref, r_ref, per_column):
    column = second // per_column - lax.axis_index("block")
    return jnp.where(column < 0, l_ref[0], jnp.where(column == 0, c_ref[0], r_ref[0]))


def near_kernel(per_column, counts, pairs, l_ref, c_ref, r_ref, w_ref, h_ref, total_ref, near_ref):
    kernels, width = w_ref.shape[0], w_ref.shape[1]
    s = pl.program_id(0)

    @pl.when(s == 0)
    def _():
        total_ref[...] = jnp.zeros_like(total_ref)

    @pl.when(s < counts[0])
    def _():
        x = near_select(pairs[s, 1], l_ref, c_ref, r_ref, per_column)
        for k in range(kernels):
            near_ref[0, :, k * width : (k + 1) * width] = dot(h_ref[0, k], x).astype(BF16)
        total_ref[pairs[s, 0]] += dot(near_ref[0], w_ref[...].reshape(kernels * width, width))


def back_near_kernel(counts, pairs, ut_ref, w_ref, near_ref, h_ref, out_ref, gd_ref, vt, gdt):
    kernels, points, width = h_ref.shape[1], h_ref.shape[2], w_ref.shape[1]
    s = pl.program_id(0)

    @pl.when(s == 0)
    def _():
        gdt[...] = jnp.zeros_like(gdt)
        for a in range(ut_ref.shape[0]):
            u = ut_ref[a]
            for k in range(kernels):
                vt[a, :, k * points : (k + 1) * points] = dot(w_ref[k], u).astype(BF16)

    @pl.when(s < counts[0])
    def _():
        a = pairs[s, 0]
        out_ref[0] = dot(vt[a], h_ref[0].reshape(kernels * points, points)).astype(BF16)
        gdt[...] += dot(ut_ref[a], near_ref[0])

    @pl.when(s == pl.num_programs(0) - 1)
    def _():
        for k in range(kernels):
            gd_ref[k] = gdt[:, k * width : (k + 1) * width].T


def back_own_kernel(
    per_column,
    counts,
    pairs,
    l_ref,
    c_ref,
    r_ref,
    mt_ref,
    wmt_ref,
    gd_ref,
    h_ref,
    total_ref,
    keep_ref,
    send_ref,
    z,
    gm,
):
    kernels, width = wmt_ref.shape[0], wmt_ref.shape[1]
    half = width // 2
    s = pl.program_id(0)

    @pl.when(s == 0)
    def _():
        total_ref[...] = jnp.zeros_like(total_ref)
        gm[...] = jnp.zeros_like(gm)

    @pl.when(s < counts[0])
    def _():
        a = pairs[s, 0]
        x = near_select(pairs[s, 1], l_ref, c_ref, r_ref, per_column)
        for k in range(kernels):
            z[:, k * width : (k + 1) * width] = dot(h_ref[0, k], x).astype(BF16)
        total_ref[a] += dot(z[...], wmt_ref[...].reshape(kernels * width, width))
        gm[...] += dot(mt_ref[a], z[...])

    @pl.when(s == pl.num_programs(0) - 1)
    def _():
        core = lax.axis_index("block") % 2
        mine = pl.multiple_of(core * half, half)
        other = pl.multiple_of((1 - core) * half, half)
        for k in range(kernels):
            at = (kernels - 1 - k) * width
            keep_ref[k] = gd_ref[k, pl.ds(mine, half)] + gm[pl.ds(mine, half), at : at + width]
            send_ref[k] = (
                gd_ref[k, pl.ds(other, half)] + gm[pl.ds(other, half), at : at + width]
            ).astype(BF16)


def in_column(code, per_column):
    block = jnp.maximum(code - 1, 0)
    here = (code > 0) & (block // per_column == lax.axis_index("block"))
    return here, block


def pick_kernel(per_column, code_l, code_c, code_r, own, up, down, far, to_l, to_c, to_r):
    blocks = own.shape[0]
    regions = per_column // blocks
    me = lax.axis_index("grp")
    for code, out in ((code_l, to_l), (code_c, to_c), (code_r, to_r)):
        for s in range(out.shape[0]):
            here, block = in_column(code[s], per_column)
            away = (block // blocks - me + 2 * regions) % regions
            local = block % blocks
            for distance, source in enumerate((own, up, far, down)):

                @pl.when(here & (away == distance))
                def _(source=source, out=out, s=s, local=local):
                    out[s] = source[local]


def merge_kernel(
    per_column, code_l, code_c, code_r, part_l, part_c, part_r, own, up, down, far, total
):
    blocks = own.shape[0]
    regions = per_column // blocks
    me = lax.axis_index("grp")
    total[...] = jnp.zeros_like(total)
    for code, part in ((code_l, part_l), (code_c, part_c), (code_r, part_r)):
        for s in range(part.shape[0]):
            here, block = in_column(code[s], per_column)
            away = (block // blocks - me + 2 * regions) % regions
            at = away * blocks + block % blocks

            @pl.when(here)
            def _(part=part, s=s, at=at):
                total[at] += part[s].astype(F32)

    own[...] = total[0:blocks]
    for distance, out in ((1, up), (2, far), (3, down)):
        out[...] = total[distance * blocks : (distance + 1) * blocks].astype(BF16)


def rows_below(count, shape):
    return lax.broadcasted_iota(jnp.int32, shape, 0) < count


def summed_rows(x, total, own, one, two, three):
    scattered = own[x] + one[x].astype(F32) + two[x].astype(F32) + three[x].astype(F32)
    return total[x] + scattered.T


def activate_kernel(counts, total, own, one, two, three, cot, act, up, upt):
    for x in range(total.shape[0]):
        rows = summed_rows(x, total, own, one, two, three)
        valid = rows_below(counts[x], rows.shape)
        pre = jnp.where(valid, rows, 0.0)
        sig = jax.nn.sigmoid(pre)
        act[x] = (pre * sig).astype(BF16)
        slope = sig * (1.0 + pre * (1.0 - sig))
        upstream = jnp.where(valid, cot[x].astype(F32) * slope, 0.0)
        up[x] = upstream.astype(BF16)
        upt[x] = upstream.T.astype(BF16)


def finish_kernel(counts, total, own, one, two, three, out):
    for x in range(total.shape[0]):
        rows = summed_rows(x, total, own, one, two, three)
        out[x] = jnp.where(rows_below(counts[x], rows.shape), rows, 0.0).astype(BF16)


def split_kernel(keep, got, own, up, down, far):
    rows = own.shape[1]
    me = lax.axis_index("grp")
    regions = keep.shape[1] // rows

    def piece(distance):
        at = pl.multiple_of((me + distance) % regions * rows, rows)
        return keep[:, pl.ds(at, rows)] + got[:, pl.ds(at, rows)].astype(F32)

    own[...] = piece(0)
    up[...] = piece(1).astype(BF16)
    far[...] = piece(2).astype(BF16)
    down[...] = piece(3).astype(BF16)


def add_kernel(own, one, two, three, out):
    total = own[...] + one[...].astype(F32) + two[...].astype(F32) + three[...].astype(F32)
    out[...] = total.astype(out.dtype)


def ordered_kernel(place, scale, own, below, above, far, out, held):
    me = place()
    held[me] = own[...]
    held[(me + 3) % 4] = below[...]
    held[(me + 1) % 4] = above[...]
    held[(me + 2) % 4] = far[...]
    total = held[0].astype(F32) + held[1].astype(F32) + held[2].astype(F32) + held[3].astype(F32)
    out[...] = (total * scale).astype(out.dtype)


def join_kernel(own, below, above, far, out):
    rows = own.shape[1]
    me = lax.axis_index("grp")
    regions = out.shape[1] // rows
    for distance, part in ((0, own), (1, above), (2, far), (3, below)):
        at = pl.multiple_of((me + distance) % regions * rows, rows)
        out[:, pl.ds(at, rows)] = part[...]


def widen_kernel(own, other, out):
    half = own.shape[1]
    core = lax.axis_index("block") % 2
    out[:, pl.ds(pl.multiple_of(core * half, half), half)] = own[...].astype(F32)
    out[:, pl.ds(pl.multiple_of((1 - core) * half, half), half)] = other[...].astype(F32)


def simple(kernel, args, outs, name, scratch=(), prefetch=0):
    single = not isinstance(outs, (list, tuple))
    outs = [outs] if single else outs
    result = call(
        kernel,
        (1,),
        prefetch,
        [whole(a.shape) for a in args[prefetch:]],
        [whole(o.shape) for o in outs],
        outs,
        list(scratch),
        name,
        size=sum(a.size * a.dtype.itemsize for a in list(args) + list(outs)),
    )(*args)
    return result[0] if single else result


def along_block(x, distance):
    peers = lax.axis_size("block")
    return lax.ppermute(
        x, "block", [(i, i + distance) for i in range(peers) if 0 <= i + distance < peers]
    )


def around_grp(x, distance):
    peers = lax.axis_size("grp")
    return lax.ppermute(x, "grp", [(i, (i + distance) % peers) for i in range(peers)])


def body(features, point_counts, kernel_weights, influence, pair_list, pair_counts, cotangent):
    blocks, points, width = features.shape
    kernels = kernel_weights.shape[0]
    slots = influence.shape[0]
    peers = lax.axis_size("block")
    regions = lax.axis_size("grp")
    per_column = blocks * regions
    flat = kernels * width
    cells = kernels * points * points
    valid = (lax.broadcasted_iota(jnp.int32, (blocks, points), 1) < point_counts[:, None])[
        ..., None
    ]
    masked = jnp.where(valid, features, jnp.zeros_like(features))
    code = jnp.where(jnp.arange(slots) < pair_counts[0], pair_list[:, 1] + 1, 0)
    code_l = along_block(code, 1)
    code_r = along_block(code, -1)
    codes = (code_l, code, code_r)

    rows_b = struct((slots, points, width), BF16)
    rows_t = struct((slots, width, points), BF16)
    own_t = struct((blocks, width, points), BF16)

    def gather_column(values):
        up, down, far = (around_grp(values, d) for d in (-1, 1, 2))
        return simple(
            functools.partial(pick_kernel, per_column),
            (*codes, values, up, down, far),
            [rows_b] * 3,
            "pick_requested",
            prefetch=3,
        )

    def gather_rest(picked):
        to_l, to_c, to_r = picked
        return along_block(to_r, 1), to_c, along_block(to_l, -1)

    def scatter(part):
        part_l, part_r = along_block(part, 1), along_block(part, -1)
        own, up, down, far = simple(
            functools.partial(merge_kernel, per_column),
            (*codes, part_l, part, part_r),
            [struct((blocks, width, points), F32)] + [own_t] * 3,
            "merge_partials",
            scratch=[pltpu.VMEM((per_column, width, points), F32)],
            prefetch=3,
        )
        return own, around_grp(up, 1), around_grp(down, -1), around_grp(far, 2)

    weight_spec = whole((kernels, width, width))
    block_spec = whole((blocks, points, width))
    turned_spec = whole((blocks, width, points))
    pair_spec = per_slot((1, kernels, points, points))
    row_spec = per_slot((1, points, width))
    part_spec = per_slot((1, width, points))
    store_spec = per_slot((1, points, flat))
    pair_flops = 2 * cells * width * slots
    pair_bytes = 2 * cells * slots
    slot_args = (pair_counts, pair_list)

    picked = gather_column(masked)
    to_second, masked_t, mirrored_t = call(
        own_kernel,
        (slots,),
        2,
        [block_spec, weight_spec, pair_spec],
        [part_spec, turned_spec, weight_spec],
        [rows_t, own_t, struct((kernels, width, width), BF16)],
        [pltpu.VMEM((blocks, width, kernels * points), BF16)],
        "own_to_second",
        pair_flops,
        pair_bytes,
    )(*slot_args, masked, kernel_weights, influence)
    near_rows = gather_rest(picked)
    scattered = scatter(to_second)
    total, near_store = call(
        functools.partial(near_kernel, per_column),
        (slots,),
        2,
        [row_spec, row_spec, row_spec, weight_spec, pair_spec],
        [block_spec, store_spec],
        [struct((blocks, points, width), F32), struct((slots, points, flat), BF16)],
        [],
        "near_to_first",
        2 * pair_flops,
        pair_bytes,
    )(*slot_args, *near_rows, kernel_weights, influence)
    activated, upstream, upstream_t = simple(
        activate_kernel,
        (point_counts, total, *scattered, cotangent),
        [struct((blocks, points, width), BF16)] * 2 + [own_t],
        "activate",
        prefetch=1,
    )

    picked = gather_column(upstream)
    to_second, grad_direct = call(
        back_near_kernel,
        (slots,),
        2,
        [turned_spec, weight_spec, store_spec, pair_spec],
        [part_spec, weight_spec],
        [rows_t, struct((kernels, width, width), F32)],
        [pltpu.VMEM((blocks, width, kernels * points), BF16), pltpu.VMEM((width, flat), F32)],
        "back_to_second",
        2 * pair_flops,
        pair_bytes,
    )(*slot_args, upstream_t, kernel_weights, near_store, influence)
    near_upstream = gather_rest(picked)
    scattered = scatter(to_second)
    half_spec = whole((kernels, width // 2, width))
    total, keep, send = call(
        functools.partial(back_own_kernel, per_column),
        (slots,),
        2,
        [row_spec, row_spec, row_spec, turned_spec, weight_spec, weight_spec, pair_spec],
        [block_spec, half_spec, half_spec],
        [
            struct((blocks, points, width), F32),
            struct((kernels, width // 2, width), F32),
            struct((kernels, width // 2, width), BF16),
        ],
        [pltpu.VMEM((points, flat), BF16), pltpu.VMEM((width, flat), F32)],
        "back_to_first",
        2 * pair_flops,
        pair_bytes,
    )(*slot_args, *near_upstream, masked_t, mirrored_t, grad_direct, influence)

    def over_block(x, partner):
        return lax.ppermute(x, "block", [(i, partner(i)) for i in range(peers)])

    def step(stride, distance):
        return lambda i: i + ((i // stride + distance) % 4 - i // stride % 4) * stride

    got = over_block(send, lambda i: i ^ 1)
    quarter = width // 2 // regions
    piece = (kernels, quarter, width)
    own, up, down, far = simple(
        split_kernel, (keep, got), [struct(piece, F32)] + [struct(piece, BF16)] * 3, "split_half"
    )
    got = around_grp(up, 1), around_grp(down, -1), around_grp(far, 2)
    summed = simple(add_kernel, (own, *got), struct(piece, BF16), "add_quarters")
    scale = 1.0 / math.sqrt(blocks * points * peers * regions)
    for stride, factor in ((2, 1.0), (8, scale)):
        got = [over_block(summed, step(stride, d)) for d in (1, -1, 2)]
        summed = simple(
            functools.partial(
                ordered_kernel, lambda n=stride: lax.axis_index("block") // n % 4, factor
            ),
            (summed, *got),
            struct(piece, BF16),
            "add_in_order",
            scratch=[pltpu.VMEM((4,) + piece, BF16)],
        )
    got = [around_grp(summed, d) for d in (1, -1, 2)]
    joined = simple(
        join_kernel, (summed, *got), struct((kernels, width // 2, width), BF16), "join_quarters"
    )
    grad_weights = simple(
        widen_kernel,
        (joined, over_block(joined, lambda i: i ^ 1)),
        struct((kernels, width, width), F32),
        "join_halves",
    )
    grad_features = simple(
        finish_kernel,
        (point_counts, total, *scattered),
        struct((blocks, points, width), BF16),
        "finish_features",
        prefetch=1,
    )
    return (activated, grad_features, grad_weights)


def solution(mesh):
    placed = (
        P(("block", "grp"), None, None),
        P(("block", "grp")),
        P(),
        P(("block", "grp"), None, None, None),
        P(("block", "grp"), None),
        P(("block", "grp")),
        P(("block", "grp"), None, None),
    )
    return jax.shard_map(
        body,
        mesh=mesh,
        in_specs=placed,
        out_specs=(P(("block", "grp"), None, None), P(("block", "grp"), None, None), P()),
        check_vma=False,
    )
```

```python
import functools
import math

import jax
import jax.numpy as jnp
from jax import lax
from jax.experimental import pallas as pl
from jax.experimental.pallas import tpu as pltpu
from jax.sharding import PartitionSpec as P

BF16 = jnp.bfloat16
F32 = jnp.float32
MIB = 1024 * 1024


def dot(a, b):
    return jnp.dot(a, b, preferred_element_type=F32)


def struct(shape, dtype):
    return jax.ShapeDtypeStruct(shape, dtype)


def run(kernel, args, outs, name, scratch=(), flops=0, outside=(), limit=20):
    single = not isinstance(outs, (list, tuple))
    outs = [outs] if single else outs
    vmem = pl.BlockSpec(memory_space=pltpu.VMEM)
    smem = pl.BlockSpec(memory_space=pltpu.SMEM)
    hbm = pl.BlockSpec(memory_space=pltpu.HBM)
    size = sum(a.size * a.dtype.itemsize for a in list(args) + list(outs))
    result = pl.pallas_call(
        kernel,
        in_specs=[
            hbm if i in outside else smem if a.dtype == jnp.int32 else vmem
            for i, a in enumerate(args)
        ],
        out_specs=[vmem] * len(outs),
        out_shape=outs,
        scratch_shapes=list(scratch),
        compiler_params=pltpu.CompilerParams(vmem_limit_bytes=limit * MIB),
        cost_estimate=pl.CostEstimate(flops=flops, bytes_accessed=size, transcendentals=0),
        name=name,
    )(*args)
    return result[0] if single else result


def decode(code, blocks):
    return code > 0, code % blocks, jnp.maximum(code // blocks - 1, 0)


def each_slot(code, blocks, work):
    def step(s, carry):
        used, first, second = decode(code[s], blocks)

        @pl.when(used)
        def _():
            work(s, first, second)

        return carry

    lax.fori_loop(0, code.shape[0], step, 0)


def own_kernel(code, m_ref, w_ref, far_h, out_ref, mt_ref, wmt_ref, h_ref, yt, arrived):
    kernels, points = h_ref.shape[1], h_ref.shape[2]
    blocks = m_ref.shape[0]

    def fetch(s):
        return pltpu.make_async_copy(far_h.at[s], h_ref.at[s], arrived.at[s])

    each_slot(code, blocks, lambda s, first, second: fetch(s).start())
    for k in range(kernels):
        wmt_ref[k] = w_ref[kernels - 1 - k].T
    for a in range(blocks):
        mt = m_ref[a].T
        mt_ref[a] = mt
        for k in range(kernels):
            yt[a, :, k * points : (k + 1) * points] = dot(wmt_ref[k], mt).astype(BF16)

    def work(s, first, second):
        fetch(s).wait()
        out_ref[s] = dot(yt[first], h_ref[s].reshape(kernels * points, points)).astype(BF16)

    each_slot(code, blocks, work)


def second_rows(s, second, per_column, chip_ref, here_ref, far_ref):
    here = lax.axis_index("block")
    column = second // per_column - here
    beside = jnp.where(column == 1 - 2 * (here % 2), chip_ref[s], far_ref[s])
    return jnp.where(column == 0, here_ref[s], beside)


def near_kernel(per_column, code, chip_ref, here_ref, far_ref, w_ref, h_ref, total_ref, near_ref):
    kernels, width = w_ref.shape[0], w_ref.shape[1]
    total_ref[...] = jnp.zeros_like(total_ref)

    def work(s, first, second):
        x = second_rows(s, second, per_column, chip_ref, here_ref, far_ref)
        for k in range(kernels):
            near_ref[s, :, k * width : (k + 1) * width] = dot(h_ref[s, k], x).astype(BF16)
        total_ref[first] += dot(near_ref[s], w_ref[...].reshape(kernels * width, width))

    each_slot(code, total_ref.shape[0], work)


def back_near_kernel(code, ut_ref, w_ref, near_ref, h_ref, out_ref, gd_ref, vt):
    kernels, points, width = h_ref.shape[1], h_ref.shape[2], w_ref.shape[1]
    blocks = ut_ref.shape[0]
    gd_ref[...] = jnp.zeros_like(gd_ref)
    for a in range(blocks):
        u = ut_ref[a]
        for k in range(kernels):
            vt[a, :, k * points : (k + 1) * points] = dot(w_ref[k], u).astype(BF16)

    def work(s, first, second):
        out_ref[s] = dot(vt[first], h_ref[s].reshape(kernels * points, points)).astype(BF16)
        gd_ref[...] += dot(ut_ref[first], near_ref[s])

    each_slot(code, blocks, work)


def back_own_kernel(
    per_column,
    code,
    chip_ref,
    here_ref,
    far_ref,
    mt_ref,
    wmt_ref,
    gd_ref,
    h_ref,
    total_ref,
    keep_ref,
    send_ref,
    z,
    gm,
):
    kernels, width = wmt_ref.shape[0], wmt_ref.shape[1]
    half = width // 2
    total_ref[...] = jnp.zeros_like(total_ref)
    gm[...] = jnp.zeros_like(gm)

    def work(s, first, second):
        x = second_rows(s, second, per_column, chip_ref, here_ref, far_ref)
        for k in range(kernels):
            z[:, k * width : (k + 1) * width] = dot(h_ref[s, k], x).astype(BF16)
        total_ref[first] += dot(z[...], wmt_ref[...].reshape(kernels * width, width))
        gm[...] += dot(mt_ref[first], z[...])

    each_slot(code, total_ref.shape[0], work)
    core = lax.axis_index("block") % 2
    for k in range(kernels):
        at = (kernels - 1 - k) * width
        both = gd_ref[:, k * width : (k + 1) * width].T + gm[:, at : at + width]
        low, high = both[:half], both[half:]
        keep_ref[k] = jnp.where(core == 0, low, high)
        send_ref[k] = jnp.where(core == 0, high, low).astype(BF16)


def pick_kernel(per_column, code_p, code_c, code_f, own, one, two, three, to_p, to_c, to_f):
    blocks = own.shape[0]
    regions = per_column // blocks
    me, column = lax.axis_index("grp"), lax.axis_index("block")
    for code, out in ((code_p, to_p), (code_c, to_c), (code_f, to_f)):
        for s in range(out.shape[0]):
            used, _, block = decode(code[s], blocks)
            here = used & (block // per_column == column)
            away = (block // blocks % regions) ^ me
            for distance, source in enumerate((own, one, two, three)):

                @pl.when(here & (away == distance))
                def _(source=source, out=out, s=s, block=block):
                    out[s] = source[block % blocks]


def merge_kernel(
    per_column, code_p, code_c, code_f, part_p, part_c, part_f, own, one, two, three, total
):
    blocks = own.shape[0]
    regions = per_column // blocks
    me, column = lax.axis_index("grp"), lax.axis_index("block")
    total[...] = jnp.zeros_like(total)
    for code, part in ((code_p, part_p), (code_c, part_c), (code_f, part_f)):
        for s in range(part.shape[0]):
            used, _, block = decode(code[s], blocks)
            away = (block // blocks % regions) ^ me
            at = away * blocks + block % blocks

            @pl.when(used & (block // per_column == column))
            def _(part=part, s=s, at=at):
                total[at] += part[s].astype(F32)

    own[...] = total[0:blocks]
    for distance, out in ((1, one), (2, two), (3, three)):
        out[...] = total[distance * blocks : (distance + 1) * blocks].astype(BF16)


def rows_below(count, shape):
    return lax.broadcasted_iota(jnp.int32, shape, 0) < count


def summed_rows(x, total, own, one, two, three):
    scattered = own[x] + one[x].astype(F32) + two[x].astype(F32) + three[x].astype(F32)
    return total[x] + scattered.T


def activate_kernel(counts, total, own, one, two, three, cot, act, up, upt):
    for x in range(total.shape[0]):
        rows = summed_rows(x, total, own, one, two, three)
        valid = rows_below(counts[x], rows.shape)
        pre = jnp.where(valid, rows, 0.0)
        sig = jax.nn.sigmoid(pre)
        act[x] = (pre * sig).astype(BF16)
        slope = sig * (1.0 + pre * (1.0 - sig))
        upstream = jnp.where(valid, cot[x].astype(F32) * slope, 0.0)
        up[x] = upstream.astype(BF16)
        upt[x] = upstream.T.astype(BF16)


def finish_kernel(counts, total, own, one, two, three, out):
    for x in range(total.shape[0]):
        rows = summed_rows(x, total, own, one, two, three)
        out[x] = jnp.where(rows_below(counts[x], rows.shape), rows, 0.0).astype(BF16)


def quarter_at(index, rows):
    return pl.ds(pl.multiple_of(index * rows, rows), rows)


def halve_kernel(keep, got, kept, sent):
    rows = kept.shape[2]
    me = lax.axis_index("grp")

    def piece(index):
        at = quarter_at(index, rows)
        return keep[:, at] + got[:, at].astype(F32)

    kept[0] = piece(me)
    kept[1] = piece(me ^ 3)
    sent[0] = piece(me ^ 1).astype(BF16)
    sent[1] = piece(me ^ 2).astype(BF16)


def quarter_kernel(pair, got, kept, sent):
    kept[...] = pair[0] + got[0].astype(F32)
    sent[...] = (pair[1] + got[1].astype(F32)).astype(BF16)


def add_kernel(scale, own, got, out):
    out[...] = ((own[...].astype(F32) + got[...].astype(F32)) * scale).astype(out.dtype)


def pair_kernel(own, got, out):
    out[0] = own[...]
    out[1] = got[...]


def join_kernel(own, got, out):
    rows = own.shape[2]
    me = lax.axis_index("grp")
    out[:, quarter_at(me, rows)] = own[0]
    out[:, quarter_at(me ^ 3, rows)] = own[1]
    out[:, quarter_at(me ^ 1, rows)] = got[0]
    out[:, quarter_at(me ^ 2, rows)] = got[1]


def widen_kernel(own, other, out):
    half = own.shape[1]
    core = lax.axis_index("block") % 2
    low, high = own[...], other[...]
    out[:, :half] = jnp.where(core == 0, low, high).astype(F32)
    out[:, half:] = jnp.where(core == 0, high, low).astype(F32)


def after(x, *earlier):
    return lax.optimization_barrier((x, *earlier))[0]


def swap(x, axis, partner):
    peers = range(lax.axis_size(axis))
    return lax.ppermute(x, axis, [(i, partner(i)) for i in peers if partner(i) in peers])


def swap_core(x):
    return swap(x, "block", lambda i: i ^ 1)


def swap_far(x):
    return swap(x, "block", lambda i: i + 1 if i % 2 else i - 1)


def swap_grp(x, bits):
    return swap(x, "grp", lambda i: i ^ bits)


def body(features, point_counts, kernel_weights, influence, pair_list, pair_counts, cotangent):
    blocks, points, width = features.shape
    kernels = kernel_weights.shape[0]
    slots = influence.shape[0]
    regions = lax.axis_size("grp")
    per_column = blocks * regions
    flat = kernels * width
    pair_flops = 2 * slots * kernels * points * points * width
    row = lax.broadcasted_iota(jnp.int32, features.shape, 1)
    masked = jnp.where(row < point_counts[:, None, None], features, jnp.zeros_like(features))
    code = (pair_list[:, 1] + 1) * blocks + pair_list[:, 0]
    code = jnp.where(jnp.arange(slots) < pair_counts[0], code, 0)

    rows_b = struct((slots, points, width), BF16)
    rows_t = struct((slots, width, points), BF16)
    own_b = struct((blocks, points, width), BF16)
    own_t = struct((blocks, width, points), BF16)
    total_b = struct((blocks, points, width), F32)

    def around(values):
        return tuple(swap_grp(values, bits) for bits in (1, 2, 3))

    received = around(masked)
    codes = (swap_core(code), code, swap_far(code))

    def exchange(values, received, part):
        part_p, part_f = swap_core(part), swap_far(part)
        to_p, to_c, to_f = run(
            functools.partial(pick_kernel, per_column),
            (*codes, after(values, part), *received),
            [rows_b] * 3,
            "pick_requested",
        )
        from_p, from_f = swap_core(to_p), swap_far(to_f)
        own, *parts = run(
            functools.partial(merge_kernel, per_column),
            (*codes, part_p, after(part, to_c), part_f),
            [struct((blocks, width, points), F32)] + [own_t] * 3,
            "merge_partials",
            scratch=[pltpu.VMEM((per_column, width, points), F32)],
        )
        scattered = (own, *(swap_grp(parts[bits - 1], bits) for bits in (1, 2, 3)))
        return (from_p, after(to_c, own), from_f), scattered

    to_second, masked_t, mirrored_t, influence = run(
        own_kernel,
        (code, masked, kernel_weights, influence),
        [rows_t, own_t, struct((kernels, width, width), BF16), struct(influence.shape, BF16)],
        "own_to_second",
        [
            pltpu.VMEM((blocks, width, kernels * points), BF16),
            pltpu.SemaphoreType.DMA((slots,)),
        ],
        pair_flops,
        outside=(3,),
        limit=31,
    )
    near_rows, scattered = exchange(masked, received, to_second)
    total, near_store = run(
        functools.partial(near_kernel, per_column),
        (code, *near_rows, kernel_weights, influence),
        [total_b, struct((slots, points, flat), BF16)],
        "near_to_first",
        [],
        2 * pair_flops,
    )
    activated, upstream, upstream_t = run(
        activate_kernel,
        (point_counts, total, *scattered, cotangent),
        [own_b, own_b, own_t],
        "activate",
    )

    received = around(upstream)
    to_second, grad_direct = run(
        back_near_kernel,
        (code, upstream_t, kernel_weights, near_store, influence),
        [rows_t, struct((width, flat), F32)],
        "back_to_second",
        [pltpu.VMEM((blocks, width, kernels * points), BF16)],
        2 * pair_flops,
    )
    near_upstream, scattered = exchange(upstream, received, to_second)
    half = (kernels, width // 2, width)
    total, keep, send = run(
        functools.partial(back_own_kernel, per_column),
        (code, *near_upstream, masked_t, mirrored_t, grad_direct, influence),
        [total_b, struct(half, F32), struct(half, BF16)],
        "back_to_first",
        [pltpu.VMEM((points, flat), BF16), pltpu.VMEM((width, flat), F32)],
        2 * pair_flops,
    )

    piece = (kernels, width // 2 // regions, width)
    pair = (2,) + piece
    got = swap_core(after(send, *scattered))
    kept, sent = run(halve_kernel, (keep, got), [struct(pair, F32), struct(pair, BF16)], "halve")
    kept, sent = run(
        quarter_kernel,
        (kept, swap_grp(sent, 1)),
        [struct(piece, F32), struct(piece, BF16)],
        "quarter",
    )

    def add(own, got, dtype, scale=1.0):
        return run(functools.partial(add_kernel, scale), (own, got), struct(piece, dtype), "add")

    summed = add(kept, swap_grp(sent, 3), BF16)
    everywhere = lax.axis_size("block") * regions * blocks * points
    for stride, bits, dtype, scale in (
        (2, 1, BF16, 1.0),
        (2, 3, F32, 1.0),
        (8, 1, F32, 1.0),
        (8, 3, BF16, 1.0 / math.sqrt(everywhere)),
    ):
        got = swap(summed, "block", lambda i, n=stride * bits: i ^ n)
        summed = add(summed, got, dtype, scale)
    two = run(pair_kernel, (summed, swap_grp(summed, 3)), struct(pair, BF16), "pair_up")
    joined = run(join_kernel, (two, swap_grp(two, 1)), struct(half, BF16), "join_quarters")
    grad_weights = run(
        widen_kernel,
        (joined, swap_core(joined)),
        struct((kernels, width, width), F32),
        "join_halves",
    )
    grad_features = run(
        finish_kernel, (point_counts, total, *scattered), own_b, "finish_features"
    )
    return (activated, grad_features, grad_weights)


def solution(mesh):
    placed = (
        P(("block", "grp"), None, None),
        P(("block", "grp")),
        P(),
        P(("block", "grp"), None, None, None),
        P(("block", "grp"), None),
        P(("block", "grp")),
        P(("block", "grp"), None, None),
    )
    return jax.shard_map(
        body,
        mesh=mesh,
        in_specs=placed,
        out_specs=(P(("block", "grp"), None, None), P(("block", "grp"), None, None), P()),
        check_vma=False,
    )
```

```python
import functools
import math

import jax
import jax.numpy as jnp
from jax import lax
from jax.experimental import pallas as pl
from jax.experimental.pallas import tpu as pltpu
from jax.sharding import PartitionSpec as P

BF16 = jnp.bfloat16
F32 = jnp.float32
MIB = 1024 * 1024


def dot(a, b):
    return jnp.dot(a, b, preferred_element_type=F32)


def struct(shape, dtype):
    return jax.ShapeDtypeStruct(shape, dtype)


def run(kernel, args, outs, name, scratch=(), flops=0, outside=(), limit=20):
    single = not isinstance(outs, (list, tuple))
    outs = [outs] if single else outs
    vmem = pl.BlockSpec(memory_space=pltpu.VMEM)
    smem = pl.BlockSpec(memory_space=pltpu.SMEM)
    hbm = pl.BlockSpec(memory_space=pltpu.HBM)
    size = sum(a.size * a.dtype.itemsize for a in list(args) + list(outs))
    result = pl.pallas_call(
        kernel,
        in_specs=[
            hbm if i in outside else smem if a.dtype == jnp.int32 else vmem
            for i, a in enumerate(args)
        ],
        out_specs=[vmem] * len(outs),
        out_shape=outs,
        scratch_shapes=list(scratch),
        compiler_params=pltpu.CompilerParams(vmem_limit_bytes=limit * MIB),
        cost_estimate=pl.CostEstimate(flops=flops, bytes_accessed=size, transcendentals=0),
        name=name,
    )(*args)
    return result[0] if single else result


def decode(code, blocks):
    return code > 0, code % blocks, jnp.maximum(code // blocks - 1, 0)


def each_slot(code, blocks, work):
    def step(s, carry):
        used, first, second = decode(code[s], blocks)

        @pl.when(used)
        def _():
            work(s, first, second)

        return carry

    lax.fori_loop(0, code.shape[0], step, 0)


def own_kernel(code, m_ref, w_ref, far_h, out_ref, mt_ref, wmt_ref, h_ref, yt, arrived):
    kernels, points = h_ref.shape[1], h_ref.shape[2]
    blocks = m_ref.shape[0]

    def fetch(s):
        return pltpu.make_async_copy(far_h.at[s], h_ref.at[s], arrived.at[s])

    each_slot(code, blocks, lambda s, first, second: fetch(s).start())
    for k in range(kernels):
        wmt_ref[k] = w_ref[kernels - 1 - k].T
    for a in range(blocks):
        mt = m_ref[a].T
        mt_ref[a] = mt
        for k in range(kernels):
            yt[a, :, k * points : (k + 1) * points] = dot(wmt_ref[k], mt).astype(BF16)

    def work(s, first, second):
        fetch(s).wait()
        out_ref[s] = dot(yt[first], h_ref[s].reshape(kernels * points, points)).astype(BF16)

    each_slot(code, blocks, work)


def second_rows(s, second, per_column, chip_ref, here_ref, far_ref):
    here = lax.axis_index("block")
    column = second // per_column - here
    beside = jnp.where(column == 1 - 2 * (here % 2), chip_ref[s], far_ref[s])
    return jnp.where(column == 0, here_ref[s], beside)


def near_kernel(per_column, code, chip_ref, here_ref, far_ref, w_ref, h_ref, total_ref, near_ref):
    kernels, width = w_ref.shape[0], w_ref.shape[1]
    total_ref[...] = jnp.zeros_like(total_ref)

    def work(s, first, second):
        x = second_rows(s, second, per_column, chip_ref, here_ref, far_ref)
        for k in range(kernels):
            near_ref[s, :, k * width : (k + 1) * width] = dot(h_ref[s, k], x).astype(BF16)
        total_ref[first] += dot(near_ref[s], w_ref[...].reshape(kernels * width, width))

    each_slot(code, total_ref.shape[0], work)


def back_near_kernel(code, ut_ref, w_ref, near_ref, h_ref, out_ref, gd_ref, vt):
    kernels, points, width = h_ref.shape[1], h_ref.shape[2], w_ref.shape[1]
    blocks = ut_ref.shape[0]
    gd_ref[...] = jnp.zeros_like(gd_ref)
    for a in range(blocks):
        u = ut_ref[a]
        for k in range(kernels):
            vt[a, :, k * points : (k + 1) * points] = dot(w_ref[k], u).astype(BF16)

    def work(s, first, second):
        out_ref[s] = dot(vt[first], h_ref[s].reshape(kernels * points, points)).astype(BF16)
        gd_ref[...] += dot(ut_ref[first], near_ref[s])

    each_slot(code, blocks, work)


def back_own_kernel(
    per_column, code, chip_ref, here_ref, far_ref, mt_ref, gd_ref, h_ref, z_ref, keep_ref, send_ref, gm
):
    kernels, width = h_ref.shape[1], here_ref.shape[2]
    half = width // 2
    gm[...] = jnp.zeros_like(gm)

    def work(s, first, second):
        x = second_rows(s, second, per_column, chip_ref, here_ref, far_ref)
        for k in range(kernels):
            z_ref[s, :, k * width : (k + 1) * width] = dot(h_ref[s, k], x).astype(BF16)
        gm[...] += dot(mt_ref[first], z_ref[s])

    each_slot(code, mt_ref.shape[0], work)
    core = lax.axis_index("block") % 2
    for k in range(kernels):
        at = (kernels - 1 - k) * width
        both = gd_ref[:, k * width : (k + 1) * width].T + gm[:, at : at + width]
        low, high = both[:half], both[half:]
        keep_ref[k] = jnp.where(core == 0, low, high)
        send_ref[k] = jnp.where(core == 0, high, low).astype(BF16)


def to_first_kernel(code, z_ref, wmt_ref, total_ref):
    kernels, width = wmt_ref.shape[0], wmt_ref.shape[1]
    total_ref[...] = jnp.zeros_like(total_ref)

    def work(s, first, second):
        total_ref[first] += dot(z_ref[s], wmt_ref[...].reshape(kernels * width, width))

    each_slot(code, total_ref.shape[0], work)


def pick_kernel(per_column, code_p, code_c, code_f, own, one, two, three, to_p, to_c, to_f):
    blocks = own.shape[0]
    regions = per_column // blocks
    me, column = lax.axis_index("grp"), lax.axis_index("block")
    for code, out in ((code_p, to_p), (code_c, to_c), (code_f, to_f)):
        for s in range(out.shape[0]):
            used, _, block = decode(code[s], blocks)
            away = (block // blocks % regions) ^ me

            @pl.when(used & (block // per_column == column))
            def _(out=out, s=s, block=block, away=away):
                for distance, source in enumerate((own, one, two, three)):

                    @pl.when(away == distance)
                    def _(source=source):
                        out[s] = source[block % blocks]


def merge_kernel(
    per_column, code_p, code_c, code_f, part_p, part_c, part_f, own, one, two, three, total
):
    blocks = own.shape[0]
    regions = per_column // blocks
    me, column = lax.axis_index("grp"), lax.axis_index("block")
    total[...] = jnp.zeros_like(total)
    for code, part in ((code_p, part_p), (code_c, part_c), (code_f, part_f)):
        for s in range(part.shape[0]):
            used, _, block = decode(code[s], blocks)
            away = (block // blocks % regions) ^ me
            at = away * blocks + block % blocks

            @pl.when(used & (block // per_column == column))
            def _(part=part, s=s, at=at):
                total[at] += part[s].astype(F32)

    own[...] = total[0:blocks]
    for distance, out in ((1, one), (2, two), (3, three)):
        out[...] = total[distance * blocks : (distance + 1) * blocks].astype(BF16)


def rows_below(count, shape):
    return lax.broadcasted_iota(jnp.int32, shape, 0) < count


def summed_rows(x, total, own, one, two, three):
    scattered = own[x] + one[x].astype(F32) + two[x].astype(F32) + three[x].astype(F32)
    return total[x] + scattered.T


def activate_kernel(counts, total, own, one, two, three, cot, act, up, upt):
    for x in range(total.shape[0]):
        rows = summed_rows(x, total, own, one, two, three)
        valid = rows_below(counts[x], rows.shape)
        pre = jnp.where(valid, rows, 0.0)
        sig = jax.nn.sigmoid(pre)
        act[x] = (pre * sig).astype(BF16)
        slope = sig * (1.0 + pre * (1.0 - sig))
        upstream = jnp.where(valid, cot[x].astype(F32) * slope, 0.0)
        up[x] = upstream.astype(BF16)
        upt[x] = upstream.T.astype(BF16)


def finish_kernel(counts, total, own, one, two, three, out):
    for x in range(total.shape[0]):
        rows = summed_rows(x, total, own, one, two, three)
        out[x] = jnp.where(rows_below(counts[x], rows.shape), rows, 0.0).astype(BF16)


def quarter_at(index, rows):
    return pl.ds(pl.multiple_of(index * rows, rows), rows)


def split_kernel(keep, got, own, one, two, three):
    rows = own.shape[1]
    me = lax.axis_index("grp")

    def piece(bits):
        at = quarter_at(me ^ bits, rows)
        return keep[:, at] + got[:, at].astype(F32)

    own[...] = piece(0)
    for bits, out in ((1, one), (2, two), (3, three)):
        out[...] = piece(bits).astype(BF16)


def add_kernel(own, one, two, three, out):
    total = own[...] + one[...].astype(F32) + two[...].astype(F32) + three[...].astype(F32)
    out[...] = total.astype(BF16)


def ordered_kernel(stride, scale, own, one, two, three, out, held):
    me = lax.axis_index("block") // stride % 4
    for bits, part in enumerate((own, one, two, three)):
        held[me ^ bits] = part[...].astype(F32)
    out[...] = ((held[0] + held[1] + held[2] + held[3]) * scale).astype(BF16)


def join_kernel(own, one, two, three, out):
    me = lax.axis_index("grp")
    for bits, part in enumerate((own, one, two, three)):
        out[:, quarter_at(me ^ bits, own.shape[1])] = part[...]


def widen_kernel(own, other, out):
    half = own.shape[1]
    core = lax.axis_index("block") % 2
    low, high = own[...], other[...]
    out[:, :half] = jnp.where(core == 0, low, high).astype(F32)
    out[:, half:] = jnp.where(core == 0, high, low).astype(F32)


def after(x, *earlier):
    return lax.optimization_barrier((x, *earlier))[0]


def swap(x, axis, partner):
    peers = range(lax.axis_size(axis))
    return lax.ppermute(x, axis, [(i, partner(i)) for i in peers if partner(i) in peers])


def swap_core(x):
    return swap(x, "block", lambda i: i ^ 1)


def swap_far(x):
    return swap(x, "block", lambda i: i + 1 if i % 2 else i - 1)


def swap_grp(x, bits):
    return swap(x, "grp", lambda i: i ^ bits)


def body(features, point_counts, kernel_weights, influence, pair_list, pair_counts, cotangent):
    blocks, points, width = features.shape
    kernels = kernel_weights.shape[0]
    slots = influence.shape[0]
    regions = lax.axis_size("grp")
    per_column = blocks * regions
    flat = kernels * width
    pair_flops = 2 * slots * kernels * points * points * width
    row = lax.broadcasted_iota(jnp.int32, features.shape, 1)
    masked = jnp.where(row < point_counts[:, None, None], features, jnp.zeros_like(features))
    code = (pair_list[:, 1] + 1) * blocks + pair_list[:, 0]
    code = jnp.where(jnp.arange(slots) < pair_counts[0], code, 0)

    rows_b = struct((slots, points, width), BF16)
    rows_t = struct((slots, width, points), BF16)
    own_b = struct((blocks, points, width), BF16)
    own_t = struct((blocks, width, points), BF16)
    total_b = struct((blocks, points, width), F32)

    def around(values):
        return tuple(swap_grp(values, bits) for bits in (1, 2, 3))

    received = around(masked)
    codes = (swap_core(code), code, swap_far(code))

    def exchange(values, received, part):
        part_p, part_f = swap_core(part), swap_far(part)
        to_p, to_c, to_f = run(
            functools.partial(pick_kernel, per_column),
            (*codes, after(values, part), *received),
            [rows_b] * 3,
            "pick_requested",
        )
        from_p, from_f = swap_core(to_p), swap_far(to_f)
        own, *parts = run(
            functools.partial(merge_kernel, per_column),
            (*codes, part_p, after(part, to_c), part_f),
            [struct((blocks, width, points), F32)] + [own_t] * 3,
            "merge_partials",
            scratch=[pltpu.VMEM((per_column, width, points), F32)],
        )
        scattered = (own, *(swap_grp(parts[bits - 1], bits) for bits in (1, 2, 3)))
        return (from_p, after(to_c, own), from_f), scattered

    to_second, masked_t, mirrored_t, influence = run(
        own_kernel,
        (code, masked, kernel_weights, influence),
        [rows_t, own_t, struct((kernels, width, width), BF16), struct(influence.shape, BF16)],
        "own_to_second",
        [
            pltpu.VMEM((blocks, width, kernels * points), BF16),
            pltpu.SemaphoreType.DMA((slots,)),
        ],
        pair_flops,
        outside=(3,),
        limit=31,
    )
    near_rows, scattered = exchange(masked, received, to_second)
    total, near_store = run(
        functools.partial(near_kernel, per_column),
        (code, *near_rows, kernel_weights, influence),
        [total_b, struct((slots, points, flat), BF16)],
        "near_to_first",
        [],
        2 * pair_flops,
    )
    activated, upstream, upstream_t = run(
        activate_kernel,
        (point_counts, total, *scattered, cotangent),
        [own_b, own_b, own_t],
        "activate",
    )

    received = around(upstream)
    to_second, grad_direct = run(
        back_near_kernel,
        (code, upstream_t, kernel_weights, near_store, influence),
        [rows_t, struct((width, flat), F32)],
        "back_to_second",
        [pltpu.VMEM((blocks, width, kernels * points), BF16)],
        2 * pair_flops,
    )
    near_upstream, scattered = exchange(upstream, received, to_second)
    half = (kernels, width // 2, width)
    piece = (kernels, width // 2 // regions, width)
    store = struct((slots, points, flat), BF16)
    z_store, keep, send = run(
        functools.partial(back_own_kernel, per_column),
        (code, *near_upstream, masked_t, grad_direct, influence),
        [store, struct(half, F32), struct(half, BF16)],
        "back_to_first",
        [pltpu.VMEM((width, flat), F32)],
        2 * pair_flops,
    )

    got = swap_core(after(send, *scattered))
    own, *parts = run(
        split_kernel, (keep, got), [struct(piece, F32)] + [struct(piece, BF16)] * 3, "split_half"
    )
    total = run(to_first_kernel, (after(code, own), z_store, mirrored_t), total_b, "to_first")
    grad_features = run(
        finish_kernel, (point_counts, total, *scattered), own_b, "finish_features"
    )
    got = [swap_grp(part, bits) for bits, part in enumerate(parts, 1)]
    summed = run(add_kernel, (after(own, total), *got), struct(piece, BF16), "add_quarters")
    everywhere = lax.axis_size("block") * regions * blocks * points
    for stride, scale in ((2, 1.0), (8, 1.0 / math.sqrt(everywhere))):
        got = [swap(summed, "block", lambda i, n=stride * b: i ^ n) for b in (1, 2, 3)]
        if stride == 2:
            summed = after(summed, grad_features)
        summed = run(
            functools.partial(ordered_kernel, stride, scale),
            (summed, *got),
            struct(piece, BF16),
            "add_in_order",
            [pltpu.VMEM((4,) + piece, F32)],
        )
    joined = run(join_kernel, (summed, *around(summed)), struct(half, BF16), "join_quarters")
    grad_weights = run(
        widen_kernel,
        (joined, swap_core(joined)),
        struct((kernels, width, width), F32),
        "join_halves",
    )
    return (activated, grad_features, grad_weights)


def solution(mesh):
    placed = (
        P(("block", "grp"), None, None),
        P(("block", "grp")),
        P(),
        P(("block", "grp"), None, None, None),
        P(("block", "grp"), None),
        P(("block", "grp")),
        P(("block", "grp"), None, None),
    )
    return jax.shard_map(
        body,
        mesh=mesh,
        in_specs=placed,
        out_specs=(P(("block", "grp"), None, None), P(("block", "grp"), None, None), P()),
        check_vma=False,
    )
```

```python
import functools
import math

import jax
import jax.numpy as jnp
from jax import lax
from jax.experimental import pallas as pl
from jax.experimental.pallas import tpu as pltpu
from jax.sharding import PartitionSpec as P

BF16 = jnp.bfloat16
F32 = jnp.float32
MIB = 1024 * 1024


def dot(a, b):
    return jnp.dot(a, b, preferred_element_type=F32)


def struct(shape, dtype):
    return jax.ShapeDtypeStruct(shape, dtype)


def run(kernel, args, outs, name, scratch=(), flops=0, outside=(), limit=20, size=None):
    single = not isinstance(outs, (list, tuple))
    outs = [outs] if single else outs
    vmem = pl.BlockSpec(memory_space=pltpu.VMEM)
    smem = pl.BlockSpec(memory_space=pltpu.SMEM)
    hbm = pl.BlockSpec(memory_space=pltpu.HBM)
    if size is None:
        size = sum(a.size * a.dtype.itemsize for a in list(args) + list(outs))
    result = pl.pallas_call(
        kernel,
        in_specs=[
            hbm if i in outside else smem if a.dtype == jnp.int32 else vmem
            for i, a in enumerate(args)
        ],
        out_specs=[vmem] * len(outs),
        out_shape=outs,
        scratch_shapes=list(scratch),
        compiler_params=pltpu.CompilerParams(vmem_limit_bytes=limit * MIB),
        cost_estimate=pl.CostEstimate(flops=flops, bytes_accessed=size, transcendentals=0),
        name=name,
    )(*args)
    return result[0] if single else result


def decode(code, blocks):
    return code > 0, code % blocks, jnp.maximum(code // blocks - 1, 0)


def each_slot(code, blocks, work):
    def step(s, carry):
        used, first, second = decode(code[s], blocks)

        @pl.when(used)
        def _():
            work(s, first, second)

        return carry

    lax.fori_loop(0, code.shape[0], step, 0)


def own_kernel(
    code, m_ref, far_w, far_h, out_ref, mt_ref, wmt_ref, h_ref, yt, w_ref, w_arrived, arrived
):
    kernels, points = h_ref.shape[1], h_ref.shape[2]
    blocks = m_ref.shape[0]

    def fetch(s):
        return pltpu.make_async_copy(far_h.at[s], h_ref.at[s], arrived.at[s])

    weights = pltpu.make_async_copy(far_w, w_ref, w_arrived)
    weights.start()
    each_slot(code, blocks, lambda s, first, second: fetch(s).start())
    weights.wait()
    for k in range(kernels):
        wmt_ref[k] = w_ref[kernels - 1 - k].T
    for a in range(blocks):
        mt = m_ref[a].T
        mt_ref[a] = mt
        for k in range(kernels):
            yt[a, :, k * points : (k + 1) * points] = dot(wmt_ref[k], mt).astype(BF16)

    def work(s, first, second):
        fetch(s).wait()
        out_ref[s] = dot(yt[first], h_ref[s].reshape(kernels * points, points)).astype(BF16)

    each_slot(code, blocks, work)


def second_rows(s, second, per_column, chip_ref, here_ref, far_ref):
    here = lax.axis_index("block")
    column = second // per_column - here
    beside = jnp.where(column == 1 - 2 * (here % 2), chip_ref[s], far_ref[s])
    return jnp.where(column == 0, here_ref[s], beside)


def near_kernel(per_column, code, chip_ref, here_ref, far_ref, w_ref, h_ref, total_ref, near_ref):
    kernels, width = w_ref.shape[0], w_ref.shape[1]
    total_ref[...] = jnp.zeros_like(total_ref)

    def work(s, first, second):
        x = second_rows(s, second, per_column, chip_ref, here_ref, far_ref)
        for k in range(kernels):
            near_ref[s, :, k * width : (k + 1) * width] = dot(h_ref[s, k], x).astype(BF16)
        total_ref[first] += dot(near_ref[s], w_ref[...].reshape(kernels * width, width))

    each_slot(code, total_ref.shape[0], work)


def back_near_kernel(code, ut_ref, w_ref, near_ref, h_ref, out_ref, gd_ref, vt):
    kernels, points, width = h_ref.shape[1], h_ref.shape[2], w_ref.shape[1]
    blocks = ut_ref.shape[0]
    gd_ref[...] = jnp.zeros_like(gd_ref)
    for a in range(blocks):
        u = ut_ref[a]
        for k in range(kernels):
            vt[a, :, k * points : (k + 1) * points] = dot(w_ref[k], u).astype(BF16)

    def work(s, first, second):
        out_ref[s] = dot(vt[first], h_ref[s].reshape(kernels * points, points)).astype(BF16)
        gd_ref[...] += dot(ut_ref[first], near_ref[s])

    each_slot(code, blocks, work)


def back_own_kernel(
    per_column, code, chip_ref, here_ref, far_ref, mt_ref, gd_ref, h_ref, z_ref, keep_ref, send_ref, gm
):
    kernels, width = h_ref.shape[1], here_ref.shape[2]
    half = width // 2
    gm[...] = jnp.zeros_like(gm)

    def work(s, first, second):
        x = second_rows(s, second, per_column, chip_ref, here_ref, far_ref)
        for k in range(kernels):
            z_ref[s, :, k * width : (k + 1) * width] = dot(h_ref[s, k], x).astype(BF16)
        gm[...] += dot(mt_ref[first], z_ref[s])

    each_slot(code, mt_ref.shape[0], work)
    core = lax.axis_index("block") % 2
    for k in range(kernels):
        at = (kernels - 1 - k) * width
        both = gd_ref[:, k * width : (k + 1) * width].T + gm[:, at : at + width]
        low, high = both[:half], both[half:]
        keep_ref[k] = jnp.where(core == 0, low, high)
        send_ref[k] = jnp.where(core == 0, high, low).astype(BF16)


def to_first_kernel(code, z_ref, wmt_ref, total_ref):
    kernels, width = wmt_ref.shape[0], wmt_ref.shape[1]
    total_ref[...] = jnp.zeros_like(total_ref)

    def work(s, first, second):
        total_ref[first] += dot(z_ref[s], wmt_ref[...].reshape(kernels * width, width))

    each_slot(code, total_ref.shape[0], work)


def pick_kernel(per_column, code_p, code_c, code_f, own, one, two, three, to_p, to_c, to_f):
    blocks = own.shape[0]
    regions = per_column // blocks
    me, column = lax.axis_index("grp"), lax.axis_index("block")
    for code, out in ((code_p, to_p), (code_c, to_c), (code_f, to_f)):
        for s in range(out.shape[0]):
            used, _, block = decode(code[s], blocks)
            away = (block // blocks % regions) ^ me

            @pl.when(used & (block // per_column == column))
            def _(out=out, s=s, block=block, away=away):
                for distance, source in enumerate((own, one, two, three)):

                    @pl.when(away == distance)
                    def _(source=source):
                        out[s] = source[block % blocks]


def merge_kernel(
    per_column, code_p, code_c, code_f, part_p, part_c, part_f, own, one, two, three, total
):
    blocks = own.shape[0]
    regions = per_column // blocks
    me, column = lax.axis_index("grp"), lax.axis_index("block")
    total[...] = jnp.zeros_like(total)
    for code, part in ((code_p, part_p), (code_c, part_c), (code_f, part_f)):
        for s in range(part.shape[0]):
            used, _, block = decode(code[s], blocks)
            away = (block // blocks % regions) ^ me
            at = away * blocks + block % blocks

            @pl.when(used & (block // per_column == column))
            def _(part=part, s=s, at=at):
                total[at] += part[s].astype(F32)

    own[...] = total[0:blocks]
    for distance, out in ((1, one), (2, two), (3, three)):
        out[...] = total[distance * blocks : (distance + 1) * blocks].astype(BF16)


def rows_below(count, shape):
    return lax.broadcasted_iota(jnp.int32, shape, 0) < count


def summed_rows(x, total, own, one, two, three):
    scattered = own[x] + one[x].astype(F32) + two[x].astype(F32) + three[x].astype(F32)
    return total[x] + scattered.T


def activate_kernel(counts, total, own, one, two, three, cot, act, up, upt):
    for x in range(total.shape[0]):
        rows = summed_rows(x, total, own, one, two, three)
        valid = rows_below(counts[x], rows.shape)
        pre = jnp.where(valid, rows, 0.0)
        sig = jax.nn.sigmoid(pre)
        act[x] = (pre * sig).astype(BF16)
        slope = sig * (1.0 + pre * (1.0 - sig))
        upstream = jnp.where(valid, cot[x].astype(F32) * slope, 0.0)
        up[x] = upstream.astype(BF16)
        upt[x] = upstream.T.astype(BF16)


def finish_kernel(counts, total, own, one, two, three, out):
    for x in range(total.shape[0]):
        rows = summed_rows(x, total, own, one, two, three)
        out[x] = jnp.where(rows_below(counts[x], rows.shape), rows, 0.0).astype(BF16)


def quarter_at(index, rows):
    return pl.ds(pl.multiple_of(index * rows, rows), rows)


def split_kernel(keep, got, own, one, two, three):
    rows = own.shape[1]
    me = lax.axis_index("grp")

    def piece(bits):
        at = quarter_at(me ^ bits, rows)
        return keep[:, at] + got[:, at].astype(F32)

    own[...] = piece(0)
    for bits, out in ((1, one), (2, two), (3, three)):
        out[...] = piece(bits).astype(BF16)


def add_kernel(own, one, two, three, out):
    total = own[...] + one[...].astype(F32) + two[...].astype(F32) + three[...].astype(F32)
    out[...] = total.astype(BF16)


def ordered_kernel(stride, scale, own, one, two, three, out, held):
    me = lax.axis_index("block") // stride % 4
    for bits, part in enumerate((own, one, two, three)):
        held[me ^ bits] = part[...].astype(F32)
    out[...] = ((held[0] + held[1] + held[2] + held[3]) * scale).astype(BF16)


def join_kernel(own, one, two, three, out):
    me = lax.axis_index("grp")
    for bits, part in enumerate((own, one, two, three)):
        out[:, quarter_at(me ^ bits, own.shape[1])] = part[...]


def widen_kernel(own, other, out):
    half = own.shape[1]
    core = lax.axis_index("block") % 2
    low, high = own[...], other[...]
    out[:, :half] = jnp.where(core == 0, low, high).astype(F32)
    out[:, half:] = jnp.where(core == 0, high, low).astype(F32)


def after(x, *earlier):
    return lax.optimization_barrier((x, *earlier))[0]


def swap(x, axis, partner):
    peers = range(lax.axis_size(axis))
    return lax.ppermute(x, axis, [(i, partner(i)) for i in peers if partner(i) in peers])


def swap_core(x):
    return swap(x, "block", lambda i: i ^ 1)


def swap_far(x):
    return swap(x, "block", lambda i: i + 1 if i % 2 else i - 1)


def swap_grp(x, bits):
    return swap(x, "grp", lambda i: i ^ bits)


def body(features, point_counts, kernel_weights, influence, pair_list, pair_counts, cotangent):
    blocks, points, width = features.shape
    kernels = kernel_weights.shape[0]
    slots = influence.shape[0]
    regions = lax.axis_size("grp")
    per_column = blocks * regions
    flat = kernels * width
    pair_flops = 2 * slots * kernels * points * points * width
    row = lax.broadcasted_iota(jnp.int32, features.shape, 1)
    masked = jnp.where(row < point_counts[:, None, None], features, jnp.zeros_like(features))
    code = (pair_list[:, 1] + 1) * blocks + pair_list[:, 0]
    code = jnp.where(jnp.arange(slots) < pair_counts[0], code, 0)

    rows_b = struct((slots, points, width), BF16)
    rows_t = struct((slots, width, points), BF16)
    own_b = struct((blocks, points, width), BF16)
    own_t = struct((blocks, width, points), BF16)
    total_b = struct((blocks, points, width), F32)

    def around(values):
        return tuple(swap_grp(values, bits) for bits in (1, 2, 3))

    received = around(masked)

    def exchange(codes, values, received, part):
        part_p, part_f = swap_core(part), swap_far(part)
        to_p, to_c, to_f = run(
            functools.partial(pick_kernel, per_column),
            (*codes, after(values, part), *received),
            [rows_b] * 3,
            "pick_requested",
        )
        from_p, from_f = swap_core(to_p), swap_far(to_f)
        own, *parts = run(
            functools.partial(merge_kernel, per_column),
            (*codes, part_p, after(part, to_c), part_f),
            [struct((blocks, width, points), F32)] + [own_t] * 3,
            "merge_partials",
            scratch=[pltpu.VMEM((per_column, width, points), F32)],
        )
        scattered = (own, *(swap_grp(parts[bits - 1], bits) for bits in (1, 2, 3)))
        return (from_p, after(to_c, own), from_f), scattered

    to_second, masked_t, mirrored_t, influence = run(
        own_kernel,
        (code, masked, kernel_weights, influence),
        [rows_t, own_t, struct((kernels, width, width), BF16), struct(influence.shape, BF16)],
        "own_to_second",
        [
            pltpu.VMEM((blocks, width, kernels * points), BF16),
            pltpu.VMEM((kernels, width, width), BF16),
            pltpu.SemaphoreType.DMA,
            pltpu.SemaphoreType.DMA((slots,)),
        ],
        pair_flops,
        outside=(2, 3),
        limit=31,
    )
    late = after(code, to_second)
    codes = (swap_core(late), code, swap_far(late))
    near_rows, scattered = exchange(codes, masked, received, to_second)
    total, near_store = run(
        functools.partial(near_kernel, per_column),
        (code, *near_rows, kernel_weights, influence),
        [total_b, struct((slots, points, flat), BF16)],
        "near_to_first",
        [],
        2 * pair_flops,
    )
    activated, upstream, upstream_t = run(
        activate_kernel,
        (point_counts, total, *scattered, cotangent),
        [own_b, own_b, own_t],
        "activate",
    )

    received = around(upstream)
    to_second, grad_direct = run(
        back_near_kernel,
        (code, upstream_t, kernel_weights, near_store, influence),
        [rows_t, struct((width, flat), F32)],
        "back_to_second",
        [pltpu.VMEM((blocks, width, kernels * points), BF16)],
        2 * pair_flops,
    )
    near_upstream, scattered = exchange(codes, upstream, received, to_second)
    half = (kernels, width // 2, width)
    piece = (kernels, width // 2 // regions, width)
    store = struct((slots, points, flat), BF16)
    z_store, keep, send = run(
        functools.partial(back_own_kernel, per_column),
        (code, *near_upstream, masked_t, grad_direct, influence),
        [store, struct(half, F32), struct(half, BF16)],
        "back_to_first",
        [pltpu.VMEM((width, flat), F32)],
        size=0,
    )

    got = swap_core(send)
    total = run(to_first_kernel, (code, z_store, mirrored_t), total_b, "to_first", size=0)
    own, *parts = run(
        split_kernel,
        (keep, after(got, total)),
        [struct(piece, F32)] + [struct(piece, BF16)] * 3,
        "split_half",
    )
    grad_features = run(
        finish_kernel, (point_counts, total, *scattered), own_b, "finish_features"
    )
    got = [swap_grp(after(part, *scattered), bits) for bits, part in enumerate(parts, 1)]
    summed = run(add_kernel, (own, *got), struct(piece, BF16), "add_quarters")
    everywhere = lax.axis_size("block") * regions * blocks * points
    for stride, scale in ((2, 1.0), (8, 1.0 / math.sqrt(everywhere))):
        got = [swap(summed, "block", lambda i, n=stride * b: i ^ n) for b in (1, 2, 3)]
        if stride == 2:
            summed = after(summed, grad_features)
        summed = run(
            functools.partial(ordered_kernel, stride, scale),
            (summed, *got),
            struct(piece, BF16),
            "add_in_order",
            [pltpu.VMEM((4,) + piece, F32)],
        )
    joined = run(join_kernel, (summed, *around(summed)), struct(half, BF16), "join_quarters")
    grad_weights = run(
        widen_kernel,
        (joined, swap_core(joined)),
        struct((kernels, width, width), F32),
        "join_halves",
    )
    return (activated, grad_features, grad_weights)


def solution(mesh):
    placed = (
        P(("block", "grp"), None, None),
        P(("block", "grp")),
        P(),
        P(("block", "grp"), None, None, None),
        P(("block", "grp"), None),
        P(("block", "grp")),
        P(("block", "grp"), None, None),
    )
    return jax.shard_map(
        body,
        mesh=mesh,
        in_specs=placed,
        out_specs=(P(("block", "grp"), None, None), P(("block", "grp"), None, None), P()),
        check_vma=False,
    )
```

```python
import functools
import math

import jax
import jax.numpy as jnp
from jax import lax
from jax.experimental import pallas as pl
from jax.experimental.pallas import tpu as pltpu
from jax.sharding import PartitionSpec as P

BF16 = jnp.bfloat16
F32 = jnp.float32
MIB = 1024 * 1024


def dot(a, b):
    return jnp.dot(a, b, preferred_element_type=F32)


def struct(shape, dtype):
    return jax.ShapeDtypeStruct(shape, dtype)


def run(kernel, args, outs, name, scratch=(), flops=0, outside=(), limit=20, size=None):
    single = not isinstance(outs, (list, tuple))
    outs = [outs] if single else outs
    vmem = pl.BlockSpec(memory_space=pltpu.VMEM)
    smem = pl.BlockSpec(memory_space=pltpu.SMEM)
    hbm = pl.BlockSpec(memory_space=pltpu.HBM)
    if size is None:
        size = sum(a.size * a.dtype.itemsize for a in list(args) + list(outs))
    result = pl.pallas_call(
        kernel,
        in_specs=[
            hbm if i in outside else smem if a.dtype == jnp.int32 else vmem
            for i, a in enumerate(args)
        ],
        out_specs=[vmem] * len(outs),
        out_shape=outs,
        scratch_shapes=list(scratch),
        compiler_params=pltpu.CompilerParams(vmem_limit_bytes=limit * MIB),
        cost_estimate=pl.CostEstimate(flops=flops, bytes_accessed=size, transcendentals=0),
        name=name,
    )(*args)
    return result[0] if single else result


def decode(code, blocks):
    return code > 0, code % blocks, jnp.maximum(code // blocks - 1, 0)


def each_slot(code, blocks, work, unused=None):
    def step(s, carry):
        used, first, second = decode(code[s], blocks)

        @pl.when(used)
        def _():
            work(s, first, second)

        if unused is not None:

            @pl.when(jnp.logical_not(used))
            def _():
                unused(s)

        return carry

    lax.fori_loop(0, code.shape[0], step, 0)


def own_kernel(code, m_ref, w_ref, far_h, out_ref, mt_ref, wmt_ref, h_ref, yt, arrived):
    kernels, points = h_ref.shape[1], h_ref.shape[2]
    blocks = m_ref.shape[0]

    def fetch(s):
        return pltpu.make_async_copy(far_h.at[s], h_ref.at[s], arrived.at[s])

    each_slot(code, blocks, lambda s, first, second: fetch(s).start())
    for k in range(kernels):
        wmt_ref[k] = w_ref[kernels - 1 - k].T
    for a in range(blocks):
        mt = m_ref[a].T
        mt_ref[a] = mt
        for k in range(kernels):
            yt[a, :, k * points : (k + 1) * points] = dot(wmt_ref[k], mt).astype(BF16)

    def work(s, first, second):
        fetch(s).wait()
        out_ref[s] = dot(yt[first], h_ref[s].reshape(kernels * points, points)).astype(BF16)

    each_slot(code, blocks, work)


def second_rows(s, second, per_column, chip_ref, here_ref, far_ref):
    here = lax.axis_index("block")
    column = second // per_column - here
    beside = jnp.where(column == 1 - 2 * (here % 2), chip_ref[s], far_ref[s])
    return jnp.where(column == 0, here_ref[s], beside)


def clear(ref, s):
    ref[s] = jnp.zeros(ref.shape[1:], ref.dtype)


def add_rows(code, terms_ref, w_ref, total_ref):
    blocks = total_ref.shape[0]
    w = w_ref[...].reshape(terms_ref.shape[2], total_ref.shape[2])
    for s in range(terms_ref.shape[0]):
        total_ref[code[s] % blocks] += dot(terms_ref[s], w)


def line_up(code, blocks_ref, line):
    blocks, _, points = blocks_ref.shape
    for s in range(code.shape[0]):
        line[:, s * points : (s + 1) * points] = blocks_ref[code[s] % blocks]


def near_kernel(per_column, code, chip_ref, here_ref, far_ref, w_ref, h_ref, total_ref, near_ref):
    kernels, width = w_ref.shape[0], w_ref.shape[1]
    total_ref[...] = jnp.zeros_like(total_ref)

    def work(s, first, second):
        x = second_rows(s, second, per_column, chip_ref, here_ref, far_ref)
        for k in range(kernels):
            near_ref[s, :, k * width : (k + 1) * width] = dot(h_ref[s, k], x).astype(BF16)
        total_ref[first] += dot(near_ref[s], w_ref[...].reshape(kernels * width, width))

    each_slot(code, total_ref.shape[0], work)


def back_near_kernel(code, ut_ref, w_ref, near_ref, h_ref, out_ref, gd_ref, vt):
    kernels, points, width = h_ref.shape[1], h_ref.shape[2], w_ref.shape[1]
    blocks = ut_ref.shape[0]
    gd_ref[...] = jnp.zeros_like(gd_ref)
    for a in range(blocks):
        u = ut_ref[a]
        for k in range(kernels):
            vt[a, :, k * points : (k + 1) * points] = dot(w_ref[k], u).astype(BF16)

    def work(s, first, second):
        out_ref[s] = dot(vt[first], h_ref[s].reshape(kernels * points, points)).astype(BF16)
        gd_ref[...] += dot(ut_ref[first], near_ref[s])

    each_slot(code, blocks, work)


def back_own_kernel(
    per_column,
    code,
    chip_ref,
    here_ref,
    far_ref,
    mt_ref,
    gd_ref,
    h_ref,
    z_ref,
    keep_ref,
    send_ref,
    gm,
    line,
):
    kernels, width = h_ref.shape[1], here_ref.shape[2]
    half = width // 2

    def work(s, first, second):
        x = second_rows(s, second, per_column, chip_ref, here_ref, far_ref)
        for k in range(kernels):
            z_ref[s, :, k * width : (k + 1) * width] = dot(h_ref[s, k], x).astype(BF16)

    each_slot(code, mt_ref.shape[0], work, functools.partial(clear, z_ref))
    line_up(code, mt_ref, line)
    gm[...] = dot(line[...], z_ref[...].reshape(-1, kernels * width))
    core = lax.axis_index("block") % 2
    for k in range(kernels):
        at = (kernels - 1 - k) * width
        both = gd_ref[:, k * width : (k + 1) * width].T + gm[:, at : at + width]
        low, high = both[:half], both[half:]
        keep_ref[k] = jnp.where(core == 0, low, high)
        send_ref[k] = jnp.where(core == 0, high, low).astype(BF16)


def to_first_kernel(code, z_ref, wmt_ref, total_ref):
    total_ref[...] = jnp.zeros_like(total_ref)
    add_rows(code, z_ref, wmt_ref, total_ref)


def pick_kernel(per_column, code_p, code_c, code_f, own, one, two, three, to_p, to_c, to_f):
    blocks = own.shape[0]
    regions = per_column // blocks
    me, column = lax.axis_index("grp"), lax.axis_index("block")
    for code, out in ((code_p, to_p), (code_c, to_c), (code_f, to_f)):
        for s in range(out.shape[0]):
            used, _, block = decode(code[s], blocks)
            away = (block // blocks % regions) ^ me

            @pl.when(used & (block // per_column == column))
            def _(out=out, s=s, block=block, away=away):
                for distance, source in enumerate((own, one, two, three)):

                    @pl.when(away == distance)
                    def _(source=source):
                        out[s] = source[block % blocks]


def merge_kernel(
    per_column, code_p, code_c, code_f, part_p, part_c, part_f, own, one, two, three, total
):
    blocks = own.shape[0]
    regions = per_column // blocks
    me, column = lax.axis_index("grp"), lax.axis_index("block")
    total[...] = jnp.zeros_like(total)
    for code, part in ((code_p, part_p), (code_c, part_c), (code_f, part_f)):
        for s in range(part.shape[0]):
            used, _, block = decode(code[s], blocks)
            away = (block // blocks % regions) ^ me
            at = away * blocks + block % blocks

            @pl.when(used & (block // per_column == column))
            def _(part=part, s=s, at=at):
                total[at] += part[s].astype(F32)

    own[...] = total[0:blocks]
    for distance, out in ((1, one), (2, two), (3, three)):
        out[...] = total[distance * blocks : (distance + 1) * blocks].astype(BF16)


def rows_below(count, shape):
    return lax.broadcasted_iota(jnp.int32, shape, 0) < count


def summed_rows(x, total, own, one, two, three):
    scattered = own[x] + one[x].astype(F32) + two[x].astype(F32) + three[x].astype(F32)
    return total[x] + scattered.T


def activate_kernel(counts, total, own, one, two, three, cot, act, up, upt):
    for x in range(total.shape[0]):
        rows = summed_rows(x, total, own, one, two, three)
        valid = rows_below(counts[x], rows.shape)
        pre = jnp.where(valid, rows, 0.0)
        sig = jax.nn.sigmoid(pre)
        act[x] = (pre * sig).astype(BF16)
        slope = sig * (1.0 + pre * (1.0 - sig))
        upstream = jnp.where(valid, cot[x].astype(F32) * slope, 0.0)
        up[x] = upstream.astype(BF16)
        upt[x] = upstream.T.astype(BF16)


def finish_kernel(counts, total, own, one, two, three, out):
    for x in range(total.shape[0]):
        rows = summed_rows(x, total, own, one, two, three)
        out[x] = jnp.where(rows_below(counts[x], rows.shape), rows, 0.0).astype(BF16)


def quarter_at(index, rows):
    return pl.ds(pl.multiple_of(index * rows, rows), rows)


def split_kernel(keep, got, own, one, two, three):
    rows = own.shape[1]
    me = lax.axis_index("grp")

    def piece(bits):
        at = quarter_at(me ^ bits, rows)
        return keep[:, at] + got[:, at].astype(F32)

    own[...] = piece(0)
    for bits, out in ((1, one), (2, two), (3, three)):
        out[...] = piece(bits).astype(BF16)


def add_kernel(own, one, two, three, out):
    total = own[...] + one[...].astype(F32) + two[...].astype(F32) + three[...].astype(F32)
    out[...] = total.astype(BF16)


def ordered_kernel(stride, scale, own, one, two, three, out, held):
    me = lax.axis_index("block") // stride % 4
    for bits, part in enumerate((own, one, two, three)):
        held[me ^ bits] = part[...].astype(F32)
    out[...] = ((held[0] + held[1] + held[2] + held[3]) * scale).astype(BF16)


def join_kernel(own, one, two, three, out):
    me = lax.axis_index("grp")
    for bits, part in enumerate((own, one, two, three)):
        out[:, quarter_at(me ^ bits, own.shape[1])] = part[...]


def widen_kernel(own, other, out):
    half = own.shape[1]
    core = lax.axis_index("block") % 2
    low, high = own[...], other[...]
    out[:, :half] = jnp.where(core == 0, low, high).astype(F32)
    out[:, half:] = jnp.where(core == 0, high, low).astype(F32)


def after(x, *earlier):
    return lax.optimization_barrier((x, *earlier))[0]


def swap(x, axis, partner):
    peers = range(lax.axis_size(axis))
    return lax.ppermute(x, axis, [(i, partner(i)) for i in peers if partner(i) in peers])


def swap_core(x):
    return swap(x, "block", lambda i: i ^ 1)


def swap_far(x):
    return swap(x, "block", lambda i: i + 1 if i % 2 else i - 1)


def swap_grp(x, bits):
    return swap(x, "grp", lambda i: i ^ bits)


def body(features, point_counts, kernel_weights, influence, pair_list, pair_counts, cotangent):
    blocks, points, width = features.shape
    kernels = kernel_weights.shape[0]
    slots = influence.shape[0]
    regions = lax.axis_size("grp")
    per_column = blocks * regions
    flat = kernels * width
    pair_flops = 2 * slots * kernels * points * points * width
    row = lax.broadcasted_iota(jnp.int32, features.shape, 1)
    masked = jnp.where(row < point_counts[:, None, None], features, jnp.zeros_like(features))
    code = (pair_list[:, 1] + 1) * blocks + pair_list[:, 0]
    code = jnp.where(jnp.arange(slots) < pair_counts[0], code, 0)

    rows_b = struct((slots, points, width), BF16)
    rows_t = struct((slots, width, points), BF16)
    own_b = struct((blocks, points, width), BF16)
    own_t = struct((blocks, width, points), BF16)
    total_b = struct((blocks, points, width), F32)

    def around(values):
        three, one, two = (swap_grp(values, bits) for bits in (3, 1, 2))
        return one, two, three

    received = around(masked)
    codes = (swap_core(code), code, swap_far(code))

    def exchange(values, received, part):
        part_p, part_f = swap_core(part), swap_far(part)
        to_p, to_c, to_f = run(
            functools.partial(pick_kernel, per_column),
            (*codes, after(values, part), *received),
            [rows_b] * 3,
            "pick_requested",
        )
        from_p, from_f = swap_core(to_p), swap_far(to_f)
        own, *parts = run(
            functools.partial(merge_kernel, per_column),
            (*codes, part_p, after(part, to_c), part_f),
            [struct((blocks, width, points), F32)] + [own_t] * 3,
            "merge_partials",
            scratch=[pltpu.VMEM((per_column, width, points), F32)],
        )
        scattered = (own, *(swap_grp(parts[bits - 1], bits) for bits in (1, 2, 3)))
        return (from_p, after(to_c, own), from_f), scattered

    line = pltpu.VMEM((width, slots * points), BF16)

    to_second, masked_t, mirrored_t, influence = run(
        own_kernel,
        (code, masked, kernel_weights, influence),
        [rows_t, own_t, struct((kernels, width, width), BF16), struct(influence.shape, BF16)],
        "own_to_second",
        [
            pltpu.VMEM((blocks, width, kernels * points), BF16),
            pltpu.SemaphoreType.DMA((slots,)),
        ],
        pair_flops,
        outside=(3,),
        limit=31,
    )
    near_rows, scattered = exchange(masked, received, to_second)
    total, near_store = run(
        functools.partial(near_kernel, per_column),
        (code, *near_rows, kernel_weights, influence),
        [total_b, struct((slots, points, flat), BF16)],
        "near_to_first",
        [],
        2 * pair_flops,
    )
    activated, upstream, upstream_t = run(
        activate_kernel,
        (point_counts, total, *scattered, cotangent),
        [own_b, own_b, own_t],
        "activate",
    )

    received = around(upstream)
    to_second, grad_direct = run(
        back_near_kernel,
        (code, upstream_t, kernel_weights, near_store, influence),
        [rows_t, struct((width, flat), F32)],
        "back_to_second",
        [pltpu.VMEM((blocks, width, kernels * points), BF16)],
        2 * pair_flops,
    )
    near_upstream, scattered = exchange(upstream, received, to_second)
    half = (kernels, width // 2, width)
    piece = (kernels, width // 2 // regions, width)
    store = struct((slots, points, flat), BF16)
    z_store, keep, send = run(
        functools.partial(back_own_kernel, per_column),
        (code, *near_upstream, masked_t, grad_direct, influence),
        [store, struct(half, F32), struct(half, BF16)],
        "back_to_first",
        [pltpu.VMEM((width, flat), F32), line],
        size=0,
    )

    got = swap_core(send)
    total = run(to_first_kernel, (code, z_store, mirrored_t), total_b, "to_first", size=0)
    own, *parts = run(
        split_kernel,
        (keep, after(got, total)),
        [struct(piece, F32)] + [struct(piece, BF16)] * 3,
        "split_half",
    )
    grad_features = run(
        finish_kernel, (point_counts, total, *scattered), own_b, "finish_features"
    )
    got = [swap_grp(after(part, *scattered), bits) for bits, part in enumerate(parts, 1)]
    summed = run(add_kernel, (own, *got), struct(piece, BF16), "add_quarters")
    everywhere = lax.axis_size("block") * regions * blocks * points
    for stride, scale in ((2, 1.0), (8, 1.0 / math.sqrt(everywhere))):
        got = [swap(summed, "block", lambda i, n=stride * b: i ^ n) for b in (1, 2, 3)]
        if stride == 2:
            summed = after(summed, grad_features)
        summed = run(
            functools.partial(ordered_kernel, stride, scale),
            (summed, *got),
            struct(piece, BF16),
            "add_in_order",
            [pltpu.VMEM((4,) + piece, F32)],
        )
    joined = run(join_kernel, (summed, *around(summed)), struct(half, BF16), "join_quarters")
    grad_weights = run(
        widen_kernel,
        (joined, swap_core(joined)),
        struct((kernels, width, width), F32),
        "join_halves",
    )
    return (activated, grad_features, grad_weights)


def solution(mesh):
    placed = (
        P(("block", "grp"), None, None),
        P(("block", "grp")),
        P(),
        P(("block", "grp"), None, None, None),
        P(("block", "grp"), None),
        P(("block", "grp")),
        P(("block", "grp"), None, None),
    )
    return jax.shard_map(
        body,
        mesh=mesh,
        in_specs=placed,
        out_specs=(P(("block", "grp"), None, None), P(("block", "grp"), None, None), P()),
        check_vma=False,
    )
```

```python
import functools
import math

import jax
import jax.numpy as jnp
from jax import lax
from jax.experimental import pallas as pl
from jax.experimental.pallas import tpu as pltpu
from jax.sharding import PartitionSpec as P

BF16 = jnp.bfloat16
F32 = jnp.float32
MIB = 1024 * 1024


def dot(a, b):
    return jnp.dot(a, b, preferred_element_type=F32)


def struct(shape, dtype):
    return jax.ShapeDtypeStruct(shape, dtype)


def run(kernel, args, outs, name, scratch=(), flops=0, outside=(), limit=20, size=None):
    single = not isinstance(outs, (list, tuple))
    outs = [outs] if single else outs
    vmem = pl.BlockSpec(memory_space=pltpu.VMEM)
    smem = pl.BlockSpec(memory_space=pltpu.SMEM)
    hbm = pl.BlockSpec(memory_space=pltpu.HBM)
    if size is None:
        size = sum(a.size * a.dtype.itemsize for a in list(args) + list(outs))
    result = pl.pallas_call(
        kernel,
        in_specs=[
            hbm if i in outside else smem if a.dtype == jnp.int32 else vmem
            for i, a in enumerate(args)
        ],
        out_specs=[vmem] * len(outs),
        out_shape=outs,
        scratch_shapes=list(scratch),
        compiler_params=pltpu.CompilerParams(vmem_limit_bytes=limit * MIB),
        cost_estimate=pl.CostEstimate(flops=flops, bytes_accessed=size, transcendentals=0),
        name=name,
    )(*args)
    return result[0] if single else result


def decode(code, blocks):
    return code > 0, code % blocks, jnp.maximum(code // blocks - 1, 0)


def each_slot(code, blocks, work, unused=None):
    def step(s, carry):
        used, first, second = decode(code[s], blocks)

        @pl.when(used)
        def _():
            work(s, first, second)

        if unused is not None:

            @pl.when(jnp.logical_not(used))
            def _():
                unused(s)

        return carry

    lax.fori_loop(0, code.shape[0], step, 0)


def own_kernel(code, m_ref, w_ref, far_h, out_ref, mt_ref, wmt_ref, h_ref, yt, arrived):
    kernels, points = h_ref.shape[1], h_ref.shape[2]
    blocks = m_ref.shape[0]

    def fetch(s):
        return pltpu.make_async_copy(far_h.at[s], h_ref.at[s], arrived.at[s])

    each_slot(code, blocks, lambda s, first, second: fetch(s).start())
    for k in range(kernels):
        wmt_ref[k] = w_ref[kernels - 1 - k].T
    for a in range(blocks):
        mt = m_ref[a].T
        mt_ref[a] = mt
        for k in range(kernels):
            yt[a, :, k * points : (k + 1) * points] = dot(wmt_ref[k], mt).astype(BF16)

    def work(s, first, second):
        fetch(s).wait()
        out_ref[s] = dot(yt[first], h_ref[s].reshape(kernels * points, points)).astype(BF16)

    each_slot(code, blocks, work)


def second_rows(s, second, per_column, chip_ref, here_ref, far_ref):
    here = lax.axis_index("block")
    column = second // per_column - here
    beside = jnp.where(column == 1 - 2 * (here % 2), chip_ref[s], far_ref[s])
    return jnp.where(column == 0, here_ref[s], beside)


def clear(ref, s):
    ref[s] = jnp.zeros(ref.shape[1:], ref.dtype)


def add_rows(code, terms_ref, w_ref, total_ref):
    blocks = total_ref.shape[0]
    w = w_ref[...].reshape(terms_ref.shape[2], total_ref.shape[2])
    for s in range(terms_ref.shape[0]):
        total_ref[code[s] % blocks] += dot(terms_ref[s], w)


def line_up(code, blocks_ref, line):
    blocks, _, points = blocks_ref.shape
    for s in range(code.shape[0]):
        line[:, s * points : (s + 1) * points] = blocks_ref[code[s] % blocks]


def near_kernel(per_column, code, chip_ref, here_ref, far_ref, w_ref, h_ref, total_ref, near_ref):
    kernels, width = w_ref.shape[0], w_ref.shape[1]
    total_ref[...] = jnp.zeros_like(total_ref)

    def work(s, first, second):
        x = second_rows(s, second, per_column, chip_ref, here_ref, far_ref)
        for k in range(kernels):
            near_ref[s, :, k * width : (k + 1) * width] = dot(h_ref[s, k], x).astype(BF16)
        total_ref[first] += dot(near_ref[s], w_ref[...].reshape(kernels * width, width))

    each_slot(code, total_ref.shape[0], work)


def back_near_kernel(code, ut_ref, w_ref, near_ref, h_ref, out_ref, gd_ref, vt, gdt):
    kernels, points, width = h_ref.shape[1], h_ref.shape[2], w_ref.shape[1]
    blocks = ut_ref.shape[0]
    gdt[...] = jnp.zeros_like(gdt)
    for a in range(blocks):
        u = ut_ref[a]
        for k in range(kernels):
            vt[a, :, k * points : (k + 1) * points] = dot(w_ref[k], u).astype(BF16)

    def work(s, first, second):
        out_ref[s] = dot(vt[first], h_ref[s].reshape(kernels * points, points)).astype(BF16)
        gdt[...] += dot(ut_ref[first], near_ref[s])

    each_slot(code, blocks, work)
    for k in range(kernels):
        gd_ref[k] = gdt[:, k * width : (k + 1) * width].T


def back_own_kernel(
    per_column,
    code,
    chip_ref,
    here_ref,
    far_ref,
    mt_ref,
    gd_ref,
    h_ref,
    z_ref,
    keep_ref,
    send_ref,
    gm,
    line,
):
    kernels, width = h_ref.shape[1], here_ref.shape[2]
    half = width // 2

    def work(s, first, second):
        x = second_rows(s, second, per_column, chip_ref, here_ref, far_ref)
        for k in range(kernels):
            z_ref[s, :, k * width : (k + 1) * width] = dot(h_ref[s, k], x).astype(BF16)

    each_slot(code, mt_ref.shape[0], work, functools.partial(clear, z_ref))
    line_up(code, mt_ref, line)
    gm[...] = dot(line[...], z_ref[...].reshape(-1, kernels * width))
    core = lax.axis_index("block") % 2
    for k in range(kernels):
        at = (kernels - 1 - k) * width
        both = gd_ref[k] + gm[:, at : at + width]
        low, high = both[:half], both[half:]
        keep_ref[k] = jnp.where(core == 0, low, high)
        send_ref[k] = jnp.where(core == 0, high, low).astype(BF16)


def to_first_kernel(code, z_ref, wmt_ref, total_ref):
    total_ref[...] = jnp.zeros_like(total_ref)
    add_rows(code, z_ref, wmt_ref, total_ref)


def pick_kernel(per_column, *refs):
    count = (len(refs) - 4) // 2
    codes, sources, outs = refs[:count], refs[count : count + 4], refs[count + 4 :]
    blocks = sources[0].shape[0]
    regions = per_column // blocks
    me, column = lax.axis_index("grp"), lax.axis_index("block")
    for code, out in zip(codes, outs):
        for s in range(out.shape[0]):
            used, _, block = decode(code[s], blocks)
            away = (block // blocks % regions) ^ me

            @pl.when(used & (block // per_column == column))
            def _(out=out, s=s, block=block, away=away):
                for distance, source in enumerate(sources):

                    @pl.when(away == distance)
                    def _(source=source):
                        out[s] = source[block % blocks]


def merge_kernel(
    per_column, code_p, code_c, code_f, part_p, part_c, part_f, own, one, two, three, total
):
    blocks = own.shape[0]
    regions = per_column // blocks
    me, column = lax.axis_index("grp"), lax.axis_index("block")
    total[...] = jnp.zeros_like(total)
    for code, part in ((code_p, part_p), (code_c, part_c), (code_f, part_f)):
        for s in range(part.shape[0]):
            used, _, block = decode(code[s], blocks)
            away = (block // blocks % regions) ^ me
            at = away * blocks + block % blocks

            @pl.when(used & (block // per_column == column))
            def _(part=part, s=s, at=at):
                total[at] += part[s].astype(F32)

    own[...] = total[0:blocks]
    for distance, out in ((1, one), (2, two), (3, three)):
        out[...] = total[distance * blocks : (distance + 1) * blocks].astype(BF16)


def rows_below(count, shape):
    return lax.broadcasted_iota(jnp.int32, shape, 0) < count


def summed_rows(x, total, own, one, two, three):
    scattered = own[x] + one[x].astype(F32) + two[x].astype(F32) + three[x].astype(F32)
    return total[x] + scattered.T


def activate_kernel(counts, total, own, one, two, three, cot, act, up, upt):
    for x in range(total.shape[0]):
        rows = summed_rows(x, total, own, one, two, three)
        valid = rows_below(counts[x], rows.shape)
        pre = jnp.where(valid, rows, 0.0)
        sig = jax.nn.sigmoid(pre)
        act[x] = (pre * sig).astype(BF16)
        slope = sig * (1.0 + pre * (1.0 - sig))
        upstream = jnp.where(valid, cot[x].astype(F32) * slope, 0.0)
        up[x] = upstream.astype(BF16)
        upt[x] = upstream.T.astype(BF16)


def finish_kernel(counts, total, own, one, two, three, out):
    for x in range(total.shape[0]):
        rows = summed_rows(x, total, own, one, two, three)
        out[x] = jnp.where(rows_below(counts[x], rows.shape), rows, 0.0).astype(BF16)


def quarter_at(index, rows):
    return pl.ds(pl.multiple_of(index * rows, rows), rows)


def split_kernel(keep, got, own, one, two, three):
    rows = own.shape[1]
    me = lax.axis_index("grp")

    def piece(bits):
        at = quarter_at(me ^ bits, rows)
        return keep[:, at] + got[:, at].astype(F32)

    own[...] = piece(0)
    for bits, out in ((1, one), (2, two), (3, three)):
        out[...] = piece(bits).astype(BF16)


def add_kernel(own, one, two, three, out):
    total = own[...] + one[...].astype(F32) + two[...].astype(F32) + three[...].astype(F32)
    out[...] = total.astype(BF16)


def ordered_kernel(stride, scale, own, one, two, three, out, held):
    me = lax.axis_index("block") // stride % 4
    for bits, part in enumerate((own, one, two, three)):
        held[me ^ bits] = part[...].astype(F32)
    out[...] = ((held[0] + held[1] + held[2] + held[3]) * scale).astype(BF16)


def join_kernel(own, one, two, three, out):
    me = lax.axis_index("grp")
    for bits, part in enumerate((own, one, two, three)):
        out[:, quarter_at(me ^ bits, own.shape[1])] = part[...]


def widen_kernel(own, other, out):
    half = own.shape[1]
    core = lax.axis_index("block") % 2
    low, high = own[...], other[...]
    out[:, :half] = jnp.where(core == 0, low, high).astype(F32)
    out[:, half:] = jnp.where(core == 0, high, low).astype(F32)


def after(x, *earlier):
    return lax.optimization_barrier((x, *earlier))[0]


def swap(x, axis, partner):
    peers = range(lax.axis_size(axis))
    return lax.ppermute(x, axis, [(i, partner(i)) for i in peers if partner(i) in peers])


def swap_core(x):
    return swap(x, "block", lambda i: i ^ 1)


def swap_far(x):
    return swap(x, "block", lambda i: i + 1 if i % 2 else i - 1)


def swap_grp(x, bits):
    return swap(x, "grp", lambda i: i ^ bits)


def body(features, point_counts, kernel_weights, influence, pair_list, pair_counts, cotangent):
    blocks, points, width = features.shape
    kernels = kernel_weights.shape[0]
    slots = influence.shape[0]
    regions = lax.axis_size("grp")
    per_column = blocks * regions
    flat = kernels * width
    pair_flops = 2 * slots * kernels * points * points * width
    row = lax.broadcasted_iota(jnp.int32, features.shape, 1)
    masked = jnp.where(row < point_counts[:, None, None], features, jnp.zeros_like(features))
    code = (pair_list[:, 1] + 1) * blocks + pair_list[:, 0]
    code = jnp.where(jnp.arange(slots) < pair_counts[0], code, 0)

    rows_b = struct((slots, points, width), BF16)
    rows_t = struct((slots, width, points), BF16)
    own_b = struct((blocks, points, width), BF16)
    own_t = struct((blocks, width, points), BF16)
    total_b = struct((blocks, points, width), F32)

    def around(values):
        three, one, two = (swap_grp(values, bits) for bits in (3, 1, 2))
        return one, two, three

    received = around(masked)
    codes = (swap_core(code), code, swap_far(code))

    def exchange(values, received, part):
        part_p, part_f = swap_core(part), swap_far(part)
        values = after(values, part)
        code_p, code_c, code_f = codes

        def pick(*asked):
            return run(
                functools.partial(pick_kernel, per_column),
                (*asked, values, *received),
                [rows_b] * len(asked),
                "pick_requested",
            )

        to_f, to_p = pick(code_f, code_p)
        from_f, from_p = swap_far(to_f), swap_core(to_p)
        own, *parts = run(
            functools.partial(merge_kernel, per_column),
            (*codes, part_p, after(part, to_f), part_f),
            [struct((blocks, width, points), F32)] + [own_t] * 3,
            "merge_partials",
            scratch=[pltpu.VMEM((per_column, width, points), F32)],
        )
        scattered = (own, *(swap_grp(parts[bits - 1], bits) for bits in (1, 2, 3)))
        (to_c,) = pick(after(code_c, own))
        return (from_p, to_c, from_f), scattered

    line = pltpu.VMEM((width, slots * points), BF16)

    to_second, masked_t, mirrored_t, influence = run(
        own_kernel,
        (code, masked, kernel_weights, influence),
        [rows_t, own_t, struct((kernels, width, width), BF16), struct(influence.shape, BF16)],
        "own_to_second",
        [
            pltpu.VMEM((blocks, width, kernels * points), BF16),
            pltpu.SemaphoreType.DMA((slots,)),
        ],
        pair_flops,
        outside=(3,),
        limit=31,
    )
    near_rows, scattered = exchange(masked, received, to_second)
    total, near_store = run(
        functools.partial(near_kernel, per_column),
        (code, *near_rows, kernel_weights, influence),
        [total_b, struct((slots, points, flat), BF16)],
        "near_to_first",
        [],
        2 * pair_flops,
    )
    activated, upstream, upstream_t = run(
        activate_kernel,
        (point_counts, total, *scattered, cotangent),
        [own_b, own_b, own_t],
        "activate",
    )

    received = around(upstream)
    to_second, grad_direct = run(
        back_near_kernel,
        (code, upstream_t, kernel_weights, near_store, influence),
        [rows_t, struct((kernels, width, width), F32)],
        "back_to_second",
        [pltpu.VMEM((blocks, width, kernels * points), BF16), pltpu.VMEM((width, flat), F32)],
        2 * pair_flops,
    )
    near_upstream, scattered = exchange(upstream, received, to_second)
    half = (kernels, width // 2, width)
    piece = (kernels, width // 2 // regions, width)
    store = struct((slots, points, flat), BF16)
    z_store, keep, send = run(
        functools.partial(back_own_kernel, per_column),
        (code, *near_upstream, masked_t, grad_direct, influence),
        [store, struct(half, F32), struct(half, BF16)],
        "back_to_first",
        [pltpu.VMEM((width, flat), F32), line],
        size=0,
    )

    got = swap_core(send)
    own, *parts = run(
        split_kernel,
        (keep, got),
        [struct(piece, F32)] + [struct(piece, BF16)] * 3,
        "split_half",
    )
    total = run(
        to_first_kernel, (after(code, own), z_store, mirrored_t), total_b, "to_first", size=0
    )
    grad_features = run(
        finish_kernel, (point_counts, total, *scattered), own_b, "finish_features"
    )
    got = [swap_grp(after(part, *scattered), bits) for bits, part in enumerate(parts, 1)]
    summed = run(add_kernel, (after(own, total), *got), struct(piece, BF16), "add_quarters")
    everywhere = lax.axis_size("block") * regions * blocks * points
    for stride, scale in ((2, 1.0), (8, 1.0 / math.sqrt(everywhere))):
        got = [swap(summed, "block", lambda i, n=stride * b: i ^ n) for b in (1, 2, 3)]
        if stride == 2:
            summed = after(summed, grad_features)
        summed = run(
            functools.partial(ordered_kernel, stride, scale),
            (summed, *got),
            struct(piece, BF16),
            "add_in_order",
            [pltpu.VMEM((4,) + piece, F32)],
        )
    joined = run(join_kernel, (summed, *around(summed)), struct(half, BF16), "join_quarters")
    grad_weights = run(
        widen_kernel,
        (joined, swap_core(joined)),
        struct((kernels, width, width), F32),
        "join_halves",
    )
    return (activated, grad_features, grad_weights)


def solution(mesh):
    placed = (
        P(("block", "grp"), None, None),
        P(("block", "grp")),
        P(),
        P(("block", "grp"), None, None, None),
        P(("block", "grp"), None),
        P(("block", "grp")),
        P(("block", "grp"), None, None),
    )
    return jax.shard_map(
        body,
        mesh=mesh,
        in_specs=placed,
        out_specs=(P(("block", "grp"), None, None), P(("block", "grp"), None, None), P()),
        check_vma=False,
    )
```

```python
import functools
import math

import jax
import jax.numpy as jnp
from jax import lax
from jax.experimental import pallas as pl
from jax.experimental.pallas import tpu as pltpu
from jax.sharding import PartitionSpec as P

BF16 = jnp.bfloat16
F32 = jnp.float32
MIB = 1024 * 1024


def dot(a, b):
    return jnp.dot(a, b, preferred_element_type=F32)


def struct(shape, dtype):
    return jax.ShapeDtypeStruct(shape, dtype)


def run(kernel, args, outs, name, scratch=(), flops=0, outside=(), limit=20, size=None):
    single = not isinstance(outs, (list, tuple))
    outs = [outs] if single else outs
    vmem = pl.BlockSpec(memory_space=pltpu.VMEM)
    smem = pl.BlockSpec(memory_space=pltpu.SMEM)
    hbm = pl.BlockSpec(memory_space=pltpu.HBM)
    if size is None:
        size = sum(a.size * a.dtype.itemsize for a in list(args) + list(outs))
    result = pl.pallas_call(
        kernel,
        in_specs=[
            hbm if i in outside else smem if a.dtype == jnp.int32 else vmem
            for i, a in enumerate(args)
        ],
        out_specs=[vmem] * len(outs),
        out_shape=outs,
        scratch_shapes=list(scratch),
        compiler_params=pltpu.CompilerParams(vmem_limit_bytes=limit * MIB),
        cost_estimate=pl.CostEstimate(flops=flops, bytes_accessed=size, transcendentals=0),
        name=name,
    )(*args)
    return result[0] if single else result


def decode(code, blocks):
    return code > 0, code % blocks, jnp.maximum(code // blocks - 1, 0)


def each_slot(code, blocks, work, unused=None):
    def step(s, carry):
        used, first, second = decode(code[s], blocks)

        @pl.when(used)
        def _():
            work(s, first, second)

        if unused is not None:

            @pl.when(jnp.logical_not(used))
            def _():
                unused(s)

        return carry

    lax.fori_loop(0, code.shape[0], step, 0)


def own_kernel(code, m_ref, w_ref, far_h, out_ref, mt_ref, wmt_ref, h_ref, yt, arrived):
    kernels, points = h_ref.shape[1], h_ref.shape[2]
    blocks = m_ref.shape[0]

    def fetch(s):
        return pltpu.make_async_copy(far_h.at[s], h_ref.at[s], arrived.at[s])

    each_slot(code, blocks, lambda s, first, second: fetch(s).start())
    for k in range(kernels):
        wmt_ref[k] = w_ref[kernels - 1 - k].T
    for a in range(blocks):
        mt = m_ref[a].T
        mt_ref[a] = mt
        for k in range(kernels):
            yt[a, :, k * points : (k + 1) * points] = dot(wmt_ref[k], mt).astype(BF16)

    def work(s, first, second):
        fetch(s).wait()
        out_ref[s] = dot(yt[first], h_ref[s].reshape(kernels * points, points)).astype(BF16)

    each_slot(code, blocks, work)


def second_rows(s, second, per_column, chip_ref, here_ref, far_ref):
    here = lax.axis_index("block")
    column = second // per_column - here
    beside = jnp.where(column == 1 - 2 * (here % 2), chip_ref[s], far_ref[s])
    return jnp.where(column == 0, here_ref[s], beside)


def clear(ref, s):
    ref[s] = jnp.zeros(ref.shape[1:], ref.dtype)


def add_rows(code, terms_ref, w_ref, total_ref):
    blocks = total_ref.shape[0]
    w = w_ref[...].reshape(terms_ref.shape[2], total_ref.shape[2])
    for s in range(terms_ref.shape[0]):
        total_ref[code[s] % blocks] += dot(terms_ref[s], w)


def line_up(code, blocks_ref, line):
    blocks, _, points = blocks_ref.shape
    for s in range(code.shape[0]):
        line[:, s * points : (s + 1) * points] = blocks_ref[code[s] % blocks]


def near_kernel(per_column, code, chip_ref, here_ref, far_ref, w_ref, h_ref, total_ref, near_ref):
    kernels, width = w_ref.shape[0], w_ref.shape[1]
    total_ref[...] = jnp.zeros_like(total_ref)

    def work(s, first, second):
        x = second_rows(s, second, per_column, chip_ref, here_ref, far_ref)
        for k in range(kernels):
            near_ref[s, :, k * width : (k + 1) * width] = dot(h_ref[s, k], x).astype(BF16)
        total_ref[first] += dot(near_ref[s], w_ref[...].reshape(kernels * width, width))

    each_slot(code, total_ref.shape[0], work)


def back_near_kernel(code, ut_ref, w_ref, near_ref, h_ref, out_ref, gd_ref, vt, gdt):
    kernels, points, width = h_ref.shape[1], h_ref.shape[2], w_ref.shape[1]
    blocks = ut_ref.shape[0]
    gdt[...] = jnp.zeros_like(gdt)
    for a in range(blocks):
        u = ut_ref[a]
        for k in range(kernels):
            vt[a, :, k * points : (k + 1) * points] = dot(w_ref[k], u).astype(BF16)

    def work(s, first, second):
        out_ref[s] = dot(vt[first], h_ref[s].reshape(kernels * points, points)).astype(BF16)
        gdt[...] += dot(ut_ref[first], near_ref[s])

    each_slot(code, blocks, work)
    for k in range(kernels):
        gd_ref[k] = gdt[:, k * width : (k + 1) * width].T


def back_own_kernel(
    per_column,
    code,
    chip_ref,
    here_ref,
    far_ref,
    mt_ref,
    gd_ref,
    h_ref,
    z_ref,
    keep_ref,
    send_ref,
    gm,
    line,
):
    kernels, width = h_ref.shape[1], here_ref.shape[2]
    half = width // 2

    def work(s, first, second):
        x = second_rows(s, second, per_column, chip_ref, here_ref, far_ref)
        for k in range(kernels):
            z_ref[s, :, k * width : (k + 1) * width] = dot(h_ref[s, k], x).astype(BF16)

    each_slot(code, mt_ref.shape[0], work, functools.partial(clear, z_ref))
    line_up(code, mt_ref, line)
    gm[...] = dot(line[...], z_ref[...].reshape(-1, kernels * width))
    core = lax.axis_index("block") % 2
    for k in range(kernels):
        at = (kernels - 1 - k) * width
        both = gd_ref[k] + gm[:, at : at + width]
        low, high = both[:half], both[half:]
        keep_ref[k] = jnp.where(core == 0, low, high)
        send_ref[k] = jnp.where(core == 0, high, low).astype(BF16)


def to_first_kernel(code, z_ref, wmt_ref, total_ref):
    total_ref[...] = jnp.zeros_like(total_ref)
    add_rows(code, z_ref, wmt_ref, total_ref)


def pick_kernel(per_column, *refs):
    count = (len(refs) - 4) // 2
    codes, sources, outs = refs[:count], refs[count : count + 4], refs[count + 4 :]
    blocks = sources[0].shape[0]
    regions = per_column // blocks
    me, column = lax.axis_index("grp"), lax.axis_index("block")
    for code, out in zip(codes, outs):
        for s in range(out.shape[0]):
            used, _, block = decode(code[s], blocks)
            away = (block // blocks % regions) ^ me

            @pl.when(used & (block // per_column == column))
            def _(out=out, s=s, block=block, away=away):
                for distance, source in enumerate(sources):

                    @pl.when(away == distance)
                    def _(source=source):
                        out[s] = source[block % blocks]


def merge_kernel(
    per_column, code_p, code_c, code_f, part_p, part_c, part_f, own, one, two, three, total
):
    blocks = own.shape[0]
    regions = per_column // blocks
    me, column = lax.axis_index("grp"), lax.axis_index("block")
    total[...] = jnp.zeros_like(total)
    for code, part in ((code_p, part_p), (code_c, part_c), (code_f, part_f)):
        for s in range(part.shape[0]):
            used, _, block = decode(code[s], blocks)
            away = (block // blocks % regions) ^ me
            at = away * blocks + block % blocks

            @pl.when(used & (block // per_column == column))
            def _(part=part, s=s, at=at):
                total[at] += part[s].astype(F32)

    own[...] = total[0:blocks]
    for distance, out in ((1, one), (2, two), (3, three)):
        out[...] = total[distance * blocks : (distance + 1) * blocks].astype(BF16)


def rows_below(count, shape):
    return lax.broadcasted_iota(jnp.int32, shape, 0) < count


def summed_rows(x, total, own, one, two, three):
    scattered = own[x] + one[x].astype(F32) + two[x].astype(F32) + three[x].astype(F32)
    return total[x] + scattered.T


def activate_kernel(counts, total, own, one, two, three, cot, act, up, upt):
    for x in range(total.shape[0]):
        rows = summed_rows(x, total, own, one, two, three)
        valid = rows_below(counts[x], rows.shape)
        pre = jnp.where(valid, rows, 0.0)
        sig = jax.nn.sigmoid(pre)
        act[x] = (pre * sig).astype(BF16)
        slope = sig * (1.0 + pre * (1.0 - sig))
        upstream = jnp.where(valid, cot[x].astype(F32) * slope, 0.0)
        up[x] = upstream.astype(BF16)
        upt[x] = upstream.T.astype(BF16)


def finish_kernel(counts, total, own, one, two, three, out):
    for x in range(total.shape[0]):
        rows = summed_rows(x, total, own, one, two, three)
        out[x] = jnp.where(rows_below(counts[x], rows.shape), rows, 0.0).astype(BF16)


def quarter_at(index, rows):
    return pl.ds(pl.multiple_of(index * rows, rows), rows)


def split_kernel(keep, got, own, one, two, three):
    rows = own.shape[1]
    me = lax.axis_index("grp")

    def piece(bits):
        at = quarter_at(me ^ bits, rows)
        return keep[:, at] + got[:, at].astype(F32)

    own[...] = piece(0)
    for bits, out in ((1, one), (2, two), (3, three)):
        out[...] = piece(bits).astype(BF16)


def add_kernel(own, one, two, three, out):
    total = own[...] + one[...].astype(F32) + two[...].astype(F32) + three[...].astype(F32)
    out[...] = total.astype(BF16)


def ordered_kernel(stride, scale, own, one, two, three, out, held):
    me = lax.axis_index("block") // stride % 4
    for bits, part in enumerate((own, one, two, three)):
        held[me ^ bits] = part[...].astype(F32)
    out[...] = ((held[0] + held[1] + held[2] + held[3]) * scale).astype(BF16)


def join_kernel(own, one, two, three, out):
    me = lax.axis_index("grp")
    for bits, part in enumerate((own, one, two, three)):
        out[:, quarter_at(me ^ bits, own.shape[1])] = part[...]


def widen_kernel(own, other, out):
    half = own.shape[1]
    core = lax.axis_index("block") % 2
    low, high = own[...], other[...]
    out[:, :half] = jnp.where(core == 0, low, high).astype(F32)
    out[:, half:] = jnp.where(core == 0, high, low).astype(F32)


def after(x, *earlier):
    return lax.optimization_barrier((x, *earlier))[0]


def swap(x, axis, partner):
    peers = range(lax.axis_size(axis))
    return lax.ppermute(x, axis, [(i, partner(i)) for i in peers if partner(i) in peers])


def swap_core(x):
    return swap(x, "block", lambda i: i ^ 1)


def swap_far(x):
    return swap(x, "block", lambda i: i + 1 if i % 2 else i - 1)


def swap_grp(x, bits):
    return swap(x, "grp", lambda i: i ^ bits)


def body(features, point_counts, kernel_weights, influence, pair_list, pair_counts, cotangent):
    blocks, points, width = features.shape
    kernels = kernel_weights.shape[0]
    slots = influence.shape[0]
    regions = lax.axis_size("grp")
    per_column = blocks * regions
    flat = kernels * width
    pair_flops = 2 * slots * kernels * points * points * width
    row = lax.broadcasted_iota(jnp.int32, features.shape, 1)
    masked = jnp.where(row < point_counts[:, None, None], features, jnp.zeros_like(features))
    code = (pair_list[:, 1] + 1) * blocks + pair_list[:, 0]
    code = jnp.where(jnp.arange(slots) < pair_counts[0], code, 0)

    rows_b = struct((slots, points, width), BF16)
    rows_t = struct((slots, width, points), BF16)
    own_b = struct((blocks, points, width), BF16)
    own_t = struct((blocks, width, points), BF16)
    total_b = struct((blocks, points, width), F32)

    def around(values):
        three, one, two = (swap_grp(values, bits) for bits in (3, 1, 2))
        return one, two, three

    received = around(masked)
    codes = (swap_core(code), code, swap_far(code))

    def exchange(values, received, part):
        part_p, part_f = swap_core(part), swap_far(part)
        values = after(values, part)
        code_p, code_c, code_f = codes

        def pick(*asked):
            return run(
                functools.partial(pick_kernel, per_column),
                (*asked, values, *received),
                [rows_b] * len(asked),
                "pick_requested",
            )

        to_f, to_p = pick(code_f, code_p)
        from_f, from_p = swap_far(to_f), swap_core(to_p)
        (to_c,) = pick(after(code_c, to_f))
        own, *parts = run(
            functools.partial(merge_kernel, per_column),
            (*codes, part_p, after(part, to_c), part_f),
            [struct((blocks, width, points), F32)] + [own_t] * 3,
            "merge_partials",
            scratch=[pltpu.VMEM((per_column, width, points), F32)],
        )
        scattered = (own, *(swap_grp(parts[bits - 1], bits) for bits in (1, 2, 3)))
        return (from_p, after(to_c, own), from_f), scattered

    line = pltpu.VMEM((width, slots * points), BF16)

    to_second, masked_t, mirrored_t, influence = run(
        own_kernel,
        (code, masked, kernel_weights, influence),
        [rows_t, own_t, struct((kernels, width, width), BF16), struct(influence.shape, BF16)],
        "own_to_second",
        [
            pltpu.VMEM((blocks, width, kernels * points), BF16),
            pltpu.SemaphoreType.DMA((slots,)),
        ],
        pair_flops,
        outside=(3,),
        limit=31,
    )
    near_rows, scattered = exchange(masked, received, to_second)
    total, near_store = run(
        functools.partial(near_kernel, per_column),
        (code, *near_rows, kernel_weights, influence),
        [total_b, struct((slots, points, flat), BF16)],
        "near_to_first",
        [],
        2 * pair_flops,
    )
    activated, upstream, upstream_t = run(
        activate_kernel,
        (point_counts, total, *scattered, cotangent),
        [own_b, own_b, own_t],
        "activate",
    )

    received = around(upstream)
    to_second, grad_direct = run(
        back_near_kernel,
        (code, upstream_t, kernel_weights, near_store, influence),
        [rows_t, struct((kernels, width, width), F32)],
        "back_to_second",
        [pltpu.VMEM((blocks, width, kernels * points), BF16), pltpu.VMEM((width, flat), F32)],
        2 * pair_flops,
    )
    near_upstream, scattered = exchange(upstream, received, to_second)
    half = (kernels, width // 2, width)
    piece = (kernels, width // 2 // regions, width)
    store = struct((slots, points, flat), BF16)
    z_store, keep, send = run(
        functools.partial(back_own_kernel, per_column),
        (code, *near_upstream, masked_t, grad_direct, influence),
        [store, struct(half, F32), struct(half, BF16)],
        "back_to_first",
        [pltpu.VMEM((width, flat), F32), line],
        size=0,
    )

    got = swap_core(send)
    own, *parts = run(
        split_kernel,
        (keep, got),
        [struct(piece, F32)] + [struct(piece, BF16)] * 3,
        "split_half",
    )
    total = run(
        to_first_kernel, (after(code, own), z_store, mirrored_t), total_b, "to_first", size=0
    )
    grad_features = run(
        finish_kernel, (point_counts, total, *scattered), own_b, "finish_features"
    )
    got = [swap_grp(after(part, *scattered), bits) for bits, part in enumerate(parts, 1)]
    summed = run(add_kernel, (after(own, total), *got), struct(piece, BF16), "add_quarters")
    everywhere = lax.axis_size("block") * regions * blocks * points
    for stride, scale in ((2, 1.0), (8, 1.0 / math.sqrt(everywhere))):
        got = [swap(summed, "block", lambda i, n=stride * b: i ^ n) for b in (1, 2, 3)]
        if stride == 2:
            summed = after(summed, grad_features)
        summed = run(
            functools.partial(ordered_kernel, stride, scale),
            (summed, *got),
            struct(piece, BF16),
            "add_in_order",
            [pltpu.VMEM((4,) + piece, F32)],
        )
    joined = run(join_kernel, (summed, *around(summed)), struct(half, BF16), "join_quarters")
    grad_weights = run(
        widen_kernel,
        (joined, swap_core(joined)),
        struct((kernels, width, width), F32),
        "join_halves",
    )
    return (activated, grad_features, grad_weights)


def solution(mesh):
    placed = (
        P(("block", "grp"), None, None),
        P(("block", "grp")),
        P(),
        P(("block", "grp"), None, None, None),
        P(("block", "grp"), None),
        P(("block", "grp")),
        P(("block", "grp"), None, None),
    )
    return jax.shard_map(
        body,
        mesh=mesh,
        in_specs=placed,
        out_specs=(P(("block", "grp"), None, None), P(("block", "grp"), None, None), P()),
        check_vma=False,
    )
```
